1024 devices in a mesh: row: 4 (over x), pitch: 64 (over y, z_lo), span: 4 (over z_hi, core).
Axes of the slice: x: 4, y: 8, z: 16 (z_hi: 2, z_lo: 8; z = z_hi * 8 + z_lo), core: 2. Of those that a mesh axis runs over, the one named last changes fastest.
Arguments:
- unknowns_array: float32 [4, 11, 5, 2048, 512], P('row', None, None, 'pitch', 'span'), may hold values from -6 to 6
- exit_spec: float32 [4, 2, 5, 5, 512], P('row', None, None, None, 'span'), may hold values from -4 to 4
- blades: int32 [4], replicated, may hold values from 24 to 96
- harmonics: int32 [4, 5], replicated, may hold values from 1 to 8
- pitch_jac: float32 [5, 5], replicated, may hold values from -2.5 to 2.5
- span_jac: float32 [5, 5], replicated, may hold values from -2.5 to 2.5
- send_cell: int32 [4, 4, 64, 256], P('row', 'span', 'pitch'), may hold values from 0 to 4095, as said below
- recv_order: int32 [4, 4, 64, 256], P('row', 'span', 'pitch'), may hold values from 0 to 255, each once within a row
Outputs:
- updated_unknowns: float32 [4, 11, 5, 2048, 512], P('row', None, None, 'pitch', 'span')
- surface_target_values: float32 [4, 4, 11, 5, 16384], P('row', 'span', None, None, 'pitch')
The draws below stay inside these ranges and needn't reach their ends.
Inputs may be any that keep to these rules, and one draw needn't show every extreme that they name: `send_cell`: within each block of one row, one span index and one pitch index the 256 entries are distinct; entries k * 4 to (k + 1) * 4 - 1 are the cells whose wall values go to the solid block of pitch index k.
All inputs are finite; a program needn't handle non-finite values.
Results may differ from the reference program's by a relative error of at most 0.0001.
Values sent between devices are 32-bit elements; how exact they have to be, the bound alone decides.
A program may use at most 64 MiB of HBM per device.

```python
import math
import jax
import jax.numpy as jnp
from jax import lax

H = 5
SNAPSHOT_COUNT = 11
QUANTITY_COUNT = 5
ANGULAR_SHARE = 32
RADIUS_SHARE = 128
HANDOFF_COUNT = 4
SURFACE_SHARE = 256
SURFACE_COUNT = 16384
CASCADE_COUNT = 4
ANGULAR_COUNT = 2048
RADIUS_COUNT = 512
N_ROW = 4
N_PITCH = 64
N_SPAN = 4


def draw_send_cell(key, part):
    blocks = N_ROW * N_SPAN * N_PITCH
    key_list = jax.random.split(jax.random.fold_in(key, 7), blocks)
    chosen = jax.vmap(lambda subkey: jax.random.permutation(subkey, ANGULAR_SHARE * RADIUS_SHARE)[:SURFACE_SHARE])(key_list)
    return chosen.reshape(N_ROW, N_SPAN, N_PITCH, SURFACE_SHARE).astype(jnp.int32)


def set_ends(values, rng, least, top_value):
    longest = values.shape.index(max(values.shape))
    spots = []
    for shift in (0, 1):
        where = [jax.random.randint(jax.random.fold_in(rng, axis), (), 0, length) for axis, length in enumerate(values.shape)]
        where[longest] = (where[longest] + shift) % values.shape[longest]
        spots.append(tuple(where))
    return values.at[spots[0]].set(least).at[spots[1]].set(top_value)


def level_of(key, shape, pieces, smallest, largest):
    loudness, own = 1.0, jax.random.fold_in(key, 6)
    for axis_at, parts in pieces:
        draws = jnp.exp(jax.random.uniform(jax.random.fold_in(own, axis_at), (parts,), jnp.float32, smallest / len(pieces), largest / len(pieces)))
        loudness = loudness * jnp.repeat(draws, shape[axis_at] // parts).reshape([-1 if axis == axis_at else 1 for axis in range(len(shape))])
    return loudness


def gaussian(own_key, extent, spread, limit, pieces=(), held_as=jnp.bfloat16):
    values = spread * jax.random.normal(own_key, extent, jnp.float32)
    if pieces:
        values = values * level_of(own_key, extent, pieces, -0.22, 0.18)
    return jnp.clip(values, -limit, limit).astype(held_as)


def setup_inputs(seed: int = 0) -> dict:
    seeds = jax.random.split(jax.random.key(seed), 9)
    unknowns_array = gaussian(seeds[0], (CASCADE_COUNT, SNAPSHOT_COUNT, QUANTITY_COUNT, ANGULAR_COUNT, RADIUS_COUNT), 1.0, 6.0, ((0, 4), (3, 64), (4, 4)), jnp.float32)
    exit_spec = gaussian(seeds[1], (CASCADE_COUNT, 2, H, QUANTITY_COUNT, RADIUS_COUNT), 0.5, 4.0, ((0, 4), (4, 4)), jnp.float32)
    blades = set_ends(jax.random.randint(seeds[2], (CASCADE_COUNT,), 24, 97), jax.random.fold_in(seeds[2], 1), 24, 96).astype(jnp.int32)
    harmonics = set_ends(jax.random.randint(seeds[3], (CASCADE_COUNT, H), 1, 9), jax.random.fold_in(seeds[3], 1), 1, 8).astype(jnp.int32)
    pitch_jac = gaussian(seeds[4], (QUANTITY_COUNT, QUANTITY_COUNT), QUANTITY_COUNT ** -0.5, 2.5, (), jnp.float32)
    span_jac = gaussian(seeds[5], (QUANTITY_COUNT, QUANTITY_COUNT), QUANTITY_COUNT ** -0.5, 2.5, (), jnp.float32)
    send_cell = draw_send_cell(jax.random.fold_in(seeds[8], 71), 0)
    recv_order = jax.vmap(lambda own: jax.random.permutation(own, SURFACE_SHARE))(jax.random.split(seeds[7], CASCADE_COUNT * N_SPAN * N_PITCH)).reshape((CASCADE_COUNT, N_SPAN, N_PITCH, SURFACE_SHARE)).astype(jnp.int32)
    return {"unknowns_array": unknowns_array, "exit_spec": exit_spec, "blades": blades, "harmonics": harmonics, "pitch_jac": pitch_jac, "span_jac": span_jac, "send_cell": send_cell, "recv_order": recv_order}


full_turn = 2.0 * math.pi
step_size = 0.25
damping = 1.0 / 16.0
coupling = 0.5
frequency = 0.5
far_weight = 0.5


def fourier_derivative_operator(count):
    index_row = jnp.arange(count, dtype=jnp.int32)
    offset = (index_row[:, None] - index_row[None, :]).astype(jnp.float32)
    nonzero = jnp.where(offset == 0, 1.0, offset)
    entries = 0.5 * frequency * jnp.cos(math.pi * offset) / jnp.sin(math.pi * nonzero / count)
    return jnp.where(offset == 0, 0.0, entries)


def interface_values(spectrum, airfoil_number, spectral_cascade_update, angular_point_number, angular_width_whole):
    snapshot_moments = jnp.arange(SNAPSHOT_COUNT, dtype=jnp.int32)
    airfoil_cycle_duration = angular_width_whole * SNAPSHOT_COUNT
    angle_shift = (spectral_cascade_update[None, None, :] * airfoil_number * angular_point_number[None, :, None] * SNAPSHOT_COUNT
             + spectral_cascade_update[None, None, :] * snapshot_moments[:, None, None] * angular_width_whole) % airfoil_cycle_duration
    angle = angle_shift.astype(jnp.float32) * (full_turn / airfoil_cycle_duration)
    table = jnp.concatenate([jnp.cos(angle), jnp.sin(angle)], axis=2)
    coeffs = spectrum.reshape(2 * H, spectrum.shape[2], spectrum.shape[3])
    return jnp.einsum("tjk,kcs->tcjs", table, coeffs, precision=lax.Precision.HIGHEST)


def advance(solution_array, pitch_ext, span_ext, heard, pitch_jac, span_jac):
    pitch_first = 0.5 * (pitch_ext[:, :, 3:-1] - pitch_ext[:, :, 1:-3])
    pitch_fourth = (pitch_ext[:, :, 4:] - 4.0 * pitch_ext[:, :, 3:-1] + 6.0 * solution_array
                    - 4.0 * pitch_ext[:, :, 1:-3] + pitch_ext[:, :, :-4])
    span_first = 0.5 * (span_ext[..., 3:-1] - span_ext[..., 1:-3])
    span_fourth = (span_ext[..., 4:] - 4.0 * span_ext[..., 3:-1] + 6.0 * solution_array
                   - 4.0 * span_ext[..., 1:-3] + span_ext[..., :-4])
    flux = jnp.einsum("ac,tcjs->tajs", pitch_jac, pitch_first, precision=lax.Precision.HIGHEST)
    flux = flux + jnp.einsum("ac,tcjs->tajs", span_jac, span_first, precision=lax.Precision.HIGHEST)
    chronological_term = jnp.einsum("ng,gwvy->nwvy", fourier_derivative_operator(SNAPSHOT_COUNT), solution_array, precision=lax.Precision.HIGHEST)
    change = flux + damping * (pitch_fourth + span_fourth) + chronological_term + coupling * (2.0 * solution_array - heard)
    return solution_array - step_size * change


def reference(unknowns_array, exit_spec, blades, harmonics, pitch_jac, span_jac, send_cell, recv_order):
    angular_width_whole = ANGULAR_SHARE * N_PITCH
    angular_point_number = jnp.arange(angular_width_whole, dtype=jnp.int32)
    faces = [interface_values(exit_spec[group], blades[group], harmonics[group], angular_point_number, angular_width_whole)
             for group in range(CASCADE_COUNT)]
    results = []
    for group in range(CASCADE_COUNT):
        solution_array = unknowns_array[group]
        heard = jnp.zeros_like(solution_array)
        for source in range(CASCADE_COUNT):
            distance = abs(source - group)
            if distance == 1:
                heard = heard + faces[source]
            elif distance >= 2:
                heard = heard + far_weight * faces[source]
        pitch_ext = jnp.concatenate([solution_array[:, :, -2:], solution_array, solution_array[:, :, :2]], axis=2)
        span_ext = jnp.pad(solution_array, ((0, 0), (0, 0), (0, 0), (2, 2)))
        results.append(advance(solution_array, pitch_ext, span_ext, heard, pitch_jac, span_jac))
    updated_unknowns = jnp.stack(results, axis=0)
    grouped_surface = updated_unknowns.reshape(CASCADE_COUNT, SNAPSHOT_COUNT, QUANTITY_COUNT, N_PITCH, ANGULAR_SHARE, N_SPAN, RADIUS_SHARE)
    grouped_surface = grouped_surface.transpose(0, 5, 3, 1, 2, 4, 6).reshape(CASCADE_COUNT, N_SPAN, N_PITCH, SNAPSHOT_COUNT, QUANTITY_COUNT, ANGULAR_SHARE * RADIUS_SHARE)
    dispatched_surface = jnp.take_along_axis(grouped_surface, send_cell[:, :, :, None, None, :], axis=5)
    dispatched_surface = dispatched_surface.reshape(CASCADE_COUNT, N_SPAN, N_PITCH, SNAPSHOT_COUNT, QUANTITY_COUNT, N_PITCH, HANDOFF_COUNT)
    delivered_surface = dispatched_surface.transpose(0, 1, 5, 3, 4, 2, 6).reshape(CASCADE_COUNT, N_SPAN, N_PITCH, SNAPSHOT_COUNT, QUANTITY_COUNT, SURFACE_SHARE)
    positioned_surface = jnp.take_along_axis(delivered_surface, recv_order[:, :, :, None, None, :], axis=5)
    surface_target_values = positioned_surface.transpose(0, 1, 3, 4, 2, 5).reshape(CASCADE_COUNT, N_SPAN, SNAPSHOT_COUNT, QUANTITY_COUNT, SURFACE_COUNT)
    return updated_unknowns, surface_target_values
```

```python
import functools
import math

import jax
import jax.numpy as jnp
import numpy as np
from jax import lax
from jax.experimental import pallas as pl
from jax.experimental.pallas import tpu as pltpu
from jax.sharding import PartitionSpec as P

MESH = pl.DeviceIdType.MESH
F32, BF16, I32 = jnp.float32, jnp.bfloat16, jnp.int32

H = 5
NT = 11
NC = 5
NJ = 32
NS = 128
NK = 256
TC = NT * NC
PAD = 64
ROWS = TC * NJ

step_size = 0.25
damping = 1.0 / 16.0
coupling = 0.5
frequency = 0.5
far_weight = 0.5

d_entries = [
    float(np.float32(0.5 * frequency * math.cos(math.pi * n) / math.sin(math.pi * n / NT)))
    for n in range(1, NT // 2 + 1)
]


def iota(shape, dim):
    return lax.broadcasted_iota(I32, shape, dim)


def split(x):
    high = x.astype(BF16)
    return high, (x - high.astype(F32)).astype(BF16)


def dot(a, b):
    return lax.dot_general(a, b, (((1,), (0,)), ((), ())), preferred_element_type=F32)


def one_hot(condition):
    return jnp.where(condition, 1.0, 0.0).astype(BF16)


def section(
    sizes,
    blades,
    harmonics,
    pitch_jac,
    span_jac,
    u_hbm,
    spec_hbm,
    cell_hbm,
    order_hbm,
    out_hbm,
    wall_ref,
    u_ref,
    upd_ref,
    heard_ref,
    specs,
    coeff_ref,
    rhs_ref,
    table_ref,
    cell_ref,
    order_ref,
    cell_s,
    cell_j,
    cell_edge,
    slot_ref,
    mix_p,
    mix_s,
    pitch_out,
    pitch_in,
    span_out,
    span_in,
    edge_ref,
    corr_ref,
    g_part,
    g_ref,
    turn_ref,
    outgoing,
    arrived,
    load_sem,
    pitch_send,
    pitch_recv,
    span_send,
    span_recv,
    row_send,
    row_recv,
    wall_send,
    wall_recv,
    out_sem,
):
    n_row, n_pitch, n_span = sizes
    handoff = NK // n_pitch
    half = handoff // 2
    r, p, s = lax.axis_index("row"), lax.axis_index("pitch"), lax.axis_index("span")

    def pitch_peer(k):
        return (r, lax.rem(p + k, n_pitch), s)

    def row_peer(k):
        return (lax.rem(r + k, n_row), p, s)

    barrier = pltpu.get_barrier_semaphore()
    span_ring = (1, n_span - 1) if n_span > 2 else (1,)
    for k in span_ring:
        pl.semaphore_signal(
            barrier, inc=1, device_id=(r, p, lax.rem(s + k, n_span)), device_id_type=MESH
        )
    for k in range(1, n_row):
        pl.semaphore_signal(barrier, inc=1, device_id=row_peer(k), device_id_type=MESH)

    def greet(k, carry):
        pl.semaphore_signal(barrier, inc=1, device_id=pitch_peer(k), device_id_type=MESH)
        return carry

    lax.fori_loop(1, n_pitch, greet, 0)

    load_u = pltpu.make_async_copy(u_hbm, u_ref, load_sem.at[0])
    load_cell = pltpu.make_async_copy(cell_hbm, cell_ref, load_sem.at[1])
    load_order = pltpu.make_async_copy(order_hbm, order_ref, load_sem.at[2])
    load_u.start()
    load_cell.start()
    load_order.start()

    lane = iota((1, NS), 1)

    pitch_out[...] = jnp.zeros_like(pitch_out)
    edge_ref[...] = jnp.zeros_like(edge_ref)
    g_ref[...] = jnp.zeros_like(g_ref)
    coeff_ref[...] = jnp.zeros_like(coeff_ref)

    @pl.when(s == 0)
    def _():
        span_in[0] = jnp.zeros_like(span_in[0])

    @pl.when(s == n_span - 1)
    def _():
        span_in[1] = jnp.zeros_like(span_in[1])

    load_u.wait()
    for layer in range(2):
        pitch_out[0, layer, 0:TC, :] = u_ref[pl.ds(NJ - 2 + layer, TC, stride=NJ), :]
        pitch_out[1, layer, 0:TC, :] = u_ref[pl.ds(layer, TC, stride=NJ), :]
    edges = jnp.zeros((TC, NS), F32)
    for j in range(NJ):
        turned = pltpu.roll(u_ref[pl.ds(j, TC, stride=NJ), :], (2 + 4 * j) % NS, 1)
        edges = jnp.where((lane >= 4 * j) & (lane < 4 * j + 4), turned, edges)
    edge_ref[0:TC, :] = edges
    e4 = lax.rem(lane, 4)
    low, high = edge_ref[0 : PAD // 2, :], edge_ref[PAD // 2 : PAD, :]
    span_out[0] = jnp.where(e4 < 2, low, pltpu.roll(high, 2, 1))
    span_out[1] = jnp.where(e4 >= 2, low, pltpu.roll(high, NS - 2, 1))

    pl.semaphore_wait(barrier, len(span_ring) + n_row - 1 + n_pitch - 1)
    right = pltpu.make_async_remote_copy(
        span_out.at[0],
        span_in.at[0],
        span_send.at[0],
        span_recv.at[0],
        device_id=(r, p, lax.rem(s + 1, n_span)),
        device_id_type=MESH,
    )
    left = pltpu.make_async_remote_copy(
        span_out.at[1],
        span_in.at[1],
        span_send.at[1],
        span_recv.at[1],
        device_id=(r, p, lax.rem(s + n_span - 1, n_span)),
        device_id_type=MESH,
    )

    @pl.when(s < n_span - 1)
    def _():
        right.start()

    @pl.when(s > 0)
    def _():
        left.start()

    halos = []
    for way, k in ((0, 1), (1, n_pitch - 1)):
        copy = pltpu.make_async_remote_copy(
            pitch_out.at[way],
            pitch_in.at[way],
            pitch_send.at[way],
            pitch_recv.at[way],
            device_id=pitch_peer(k),
            device_id_type=MESH,
        )
        copy.start()
        halos.append(copy)
    spectra = []
    for k in range(1, n_row):
        copy = pltpu.make_async_remote_copy(
            spec_hbm,
            specs.at[r],
            row_send.at[k],
            row_recv,
            device_id=row_peer(k),
            device_id_type=MESH,
        )
        copy.start()
        spectra.append(copy)
    pltpu.make_async_copy(spec_hbm, specs.at[r], row_recv).start()

    load_cell.wait()
    load_order.wait()
    cell = cell_ref[...]
    cj, cs = cell // NS, lax.rem(cell, NS)
    cell_s[...] = one_hot((iota((2 * NS, NK), 0) & (NS - 1)) == cs)
    cell_j[...] = jnp.where(iota((NJ, NK), 0) == cj, 1.0, 0.0)
    place = iota((2 * NS, NK), 0) & (NS - 1)
    e_row = place & 3
    column = jnp.where(e_row < 2, e_row, NS - 4 + e_row)
    cell_edge[...] = one_hot((place // 4 == cj) & (column == cs))
    rho = iota((NK, NK), 0)
    rest = rho & (NS - 1)
    slot = (rest & (n_pitch - 1)) * handoff + (rest // n_pitch) * 2 + rho // NS
    slot_ref[...] = one_hot(slot == order_ref[...])

    mr, mc = iota((PAD, NS), 0), iota((PAD, NS), 1) & (PAD - 1)
    tr, tcol = (mr * 205) >> 10, (mc * 205) >> 10
    cr, cc = mr - 5 * tr, mc - 5 * tcol
    same = (tr == tcol) & (mr < TC) & (mc < TC)
    pair = jnp.where(same, cr * NC + cc, -1)
    for jac, mix in ((pitch_jac, mix_p), (span_jac, mix_s)):
        m = jnp.zeros((PAD, NS), F32)
        for a in range(NC):
            for c in range(NC):
                m = jnp.where(pair == a * NC + c, jac[a, c], m)
        mh, ml = split(m)
        mix[:, 0:NS] = mh
        mix[:, NS : 2 * NS] = ml

    l64 = lane & (PAD - 1)
    lg, lk = l64 // 16, l64 & 15
    order_of = jnp.zeros((1, NS), I32)
    turns_of = jnp.zeros((1, NS), I32)
    weight = jnp.zeros((1, NS), F32)
    for g in range(n_row):
        distance = jnp.abs(r - g)
        w = jnp.where(distance == 1, 1.0, jnp.where(distance >= 2, far_weight, 0.0)).astype(F32)
        weight = jnp.where((lg == g) & (lk < 2 * H), w, weight)
        for n in range(H):
            here = (lg == g) & (lk // 2 == n)
            order_of = jnp.where(here, harmonics[g, n], order_of)
            turns_of = jnp.where(here, harmonics[g, n] * blades[g], turns_of)
    whole = n_pitch * NJ
    cells = p * NJ + iota((NJ, NS), 0)
    phase_j = ((turns_of * cells) & (whole - 1)).astype(F32) * (2.0 * math.pi / whole)
    phase_j = phase_j - (lk & 1).astype(F32) * (0.5 * math.pi)
    times = order_of * iota((16, NS), 0)
    times = times - NT * ((times * 5958) >> 16)
    phase_t = times.astype(F32) * (2.0 * math.pi / NT)
    cos_j, sin_j = weight * jnp.cos(phase_j), weight * jnp.sin(phase_j)
    cos_t, sin_t = jnp.cos(phase_t), jnp.sin(phase_t)
    for t in range(NT):
        high, low = split(cos_t[t : t + 1] * cos_j - sin_t[t : t + 1] * sin_j)
        table_ref[t * NJ : (t + 1) * NJ, 0:NS] = high
        table_ref[t * NJ : (t + 1) * NJ, NS : 2 * NS] = low

    row = iota((1, NJ, 1), 1)

    def at(t):
        return pl.ds(pl.multiple_of(t * (NC * NJ), NC * NJ), NC * NJ)

    def interior(t, carry):
        x = u_ref[at(t), :]
        m1 = jnp.where(lane >= 1, pltpu.roll(x, 1, 1), 0.0)
        m2 = jnp.where(lane >= 2, pltpu.roll(x, 2, 1), 0.0)
        p1 = jnp.where(lane < NS - 1, pltpu.roll(x, NS - 1, 1), 0.0)
        p2 = jnp.where(lane < NS - 2, pltpu.roll(x, NS - 2, 1), 0.0)
        d1s = (0.5 * (p1 - m1)).reshape(NC, NJ, NS)
        fourth = ((p2 + m2) - 4.0 * (p1 + m1)).reshape(NC, NJ, NS)
        x = x.reshape(NC, NJ, NS)
        m1 = jnp.where(row >= 1, pltpu.roll(x, 1, 1), 0.0)
        m2 = jnp.where(row >= 2, pltpu.roll(x, 2, 1), 0.0)
        p1 = jnp.where(row < NJ - 1, pltpu.roll(x, NJ - 1, 1), 0.0)
        p2 = jnp.where(row < NJ - 2, pltpu.roll(x, NJ - 2, 1), 0.0)
        d1p = 0.5 * (p1 - m1)
        fourth = fourth + ((p2 + m2) - 4.0 * (p1 + m1))
        change = damping * fourth + (12.0 * damping + 2.0 * coupling) * x
        for n in range(1, NT // 2 + 1):
            before = u_ref[at(lax.rem(t + NT - n, NT)), :]
            after = u_ref[at(lax.rem(t + n, NT)), :]
            change = change + d_entries[n - 1] * (before - after).reshape(NC, NJ, NS)
        for a in range(NC):
            flux = change[a]
            for c in range(NC):
                flux = flux + pitch_jac[a, c] * d1p[c] + span_jac[a, c] * d1s[c]
            upd_ref[pl.ds(pl.multiple_of((t * NC + a) * NJ, NJ), NJ), :] = x[a] - step_size * flux
        return carry

    lax.fori_loop(0, NT, interior, 0)

    pltpu.make_async_copy(specs, specs, row_recv).wait()
    for g in range(n_row):
        for n in range(H):
            for c in range(NC):
                coeff_ref[16 * g + 2 * n : 16 * g + 2 * n + 2, c * NS : (c + 1) * NS] = specs[
                    g, n * NC + c
                ]
    high, low = split(coeff_ref[...])
    for k in range(2):
        rhs_ref[2 * PAD * k : 2 * PAD * k + PAD, :] = high
        rhs_ref[2 * PAD * k + PAD : 2 * PAD * (k + 1), :] = low
    heard_ref[...] = dot(table_ref[...], rhs_ref[...])

    def gather(t, carry):
        heard = heard_ref[pl.ds(pl.multiple_of(t * NJ, NJ), NJ), :]
        heard = jnp.concatenate([heard[:, c * NS : (c + 1) * NS] for c in range(NC)], axis=0)
        x = upd_ref[at(t), :] + (step_size * coupling) * heard
        upd_ref[at(t), :] = x
        high, low = split(x)
        found = dot(jnp.concatenate([high, low], axis=1), cell_s[...])
        found = found.reshape(NC, NJ, NK) * cell_j[...]
        g_part[t] = jnp.sum(found, axis=1)
        return carry

    lax.fori_loop(0, NT, gather, 0)
    for t in range(NT):
        g_ref[t * NC : (t + 1) * NC, :] = g_part[t]

    @pl.when(s < n_span - 1)
    def _():
        left_in = pltpu.make_async_copy(span_in.at[1], span_in.at[1], span_recv.at[1])
        left_in.wait()

    @pl.when(s > 0)
    def _():
        right_in = pltpu.make_async_copy(span_in.at[0], span_in.at[0], span_recv.at[0])
        right_in.wait()

    from_left, from_right = span_in[0], span_in[1]
    x = jnp.concatenate(
        [
            jnp.where(e4 < 2, from_left, from_right),
            jnp.where(e4 < 2, pltpu.roll(from_left, NS - 2, 1), pltpu.roll(from_right, 2, 1)),
        ],
        axis=0,
    )
    y = jnp.where(e4 == 0, pltpu.roll(x, NS - 1, 1), jnp.where(e4 == 3, pltpu.roll(x, 1, 1), 0.0))
    sign = jnp.where(e4 == 0, -0.5, jnp.where(e4 == 3, 0.5, 0.0))
    high, low = split(y)
    mixed = dot(mix_s[...], jnp.concatenate([high, low, high, low], axis=0))
    corr_ref[4] = -step_size * (sign * mixed + damping * (x - 4.0 * y))

    for copy in halos:
        copy.wait_recv()
    inner = jnp.concatenate([pitch_in[0, 1], pitch_in[1, 0]], axis=1)
    high, low = split(inner)
    mixed = dot(mix_p[...], jnp.concatenate([high, low, high, low], axis=0))
    corr_ref[0] = -step_size * (
        -0.5 * mixed[:, 0:NS] + damping * (pitch_in[0, 0] - 4.0 * pitch_in[0, 1])
    )
    corr_ref[1] = (-step_size * damping) * pitch_in[0, 1]
    corr_ref[2] = (-step_size * damping) * pitch_in[1, 0]
    corr_ref[3] = -step_size * (
        0.5 * mixed[:, NS : 2 * NS] + damping * (pitch_in[1, 1] - 4.0 * pitch_in[1, 0])
    )

    high, low = split(corr_ref[4])
    total = g_ref[...] + dot(jnp.concatenate([high, low], axis=1), cell_edge[...])
    high, low = split(corr_ref[0:4].reshape(4 * PAD, NS))
    found = dot(jnp.concatenate([high, low], axis=1), cell_s[...])
    for e, at_row in enumerate((0, 1, NJ - 2, NJ - 1)):
        total = total + found[e * PAD : (e + 1) * PAD] * cell_j[at_row : at_row + 1, :]

    turn_ref[...] = jnp.concatenate([total, pltpu.roll(total, NK - 1, 1)], axis=0).T
    for i in range(half):
        outgoing[:, i, :] = turn_ref[pl.ds(2 * i, n_pitch, stride=handoff), :]

    def send(k, carry):
        q = lax.rem(p + k, n_pitch)
        pltpu.make_async_remote_copy(
            outgoing.at[q],
            arrived.at[p],
            wall_send,
            wall_recv,
            device_id=(r, q, s),
            device_id_type=MESH,
        ).start()
        return carry

    lax.fori_loop(1, n_pitch, send, 0)
    pltpu.make_async_copy(outgoing.at[p], arrived.at[p], wall_recv).start()

    for e, at_row in enumerate((0, 1, NJ - 2, NJ - 1)):
        rows = pl.ds(at_row, TC, stride=NJ)
        upd_ref[rows, :] = upd_ref[rows, :] + corr_ref[e, 0:TC, :]
    e_lane = iota((2 * NS, NS), 0) & 3
    to_column = one_hot(iota((2 * NS, NS), 1) == jnp.where(e_lane < 2, e_lane, NS - 4 + e_lane))
    own = lane // 4 == iota((NJ, NS), 0)
    for t in range(NT):
        spread = jnp.concatenate(
            [
                jnp.where(own, corr_ref[4, t * NC + c : t * NC + c + 1, :], 0.0)
                for c in range(NC)
            ],
            axis=0,
        )
        high, low = split(spread)
        rows = slice(t * NC * NJ, (t + 1) * NC * NJ)
        upd_ref[rows, :] = upd_ref[rows, :] + dot(
            jnp.concatenate([high, low], axis=1), to_column
        )
    store = pltpu.make_async_copy(upd_ref, out_hbm, out_sem)
    store.start()

    pltpu.make_async_copy(arrived, arrived, wall_recv).wait()
    slots = jnp.concatenate([arrived[:, i, :] for i in range(half)], axis=0).T
    high, low = split(jnp.concatenate([slots[0:PAD], slots[PAD : 2 * PAD]], axis=1))
    placed = dot(jnp.concatenate([high, low], axis=0), slot_ref[...])
    placed = placed[0:PAD] + placed[PAD : 2 * PAD]
    for k in range(NK // NS):
        wall_ref[:, k, :] = placed[0:TC, k * NS : (k + 1) * NS]

    some = outgoing.at[pl.ds(0, n_pitch - 1)]
    pltpu.make_async_copy(some, some, wall_send).wait()
    for copy in halos + spectra:
        copy.wait_send()

    @pl.when(s < n_span - 1)
    def _():
        right.wait_send()

    @pl.when(s > 0)
    def _():
        left.wait_send()

    store.wait()


def local(sizes, unknowns, spectrum, blades, harmonics, pitch_jac, span_jac, send_cell, recv_order):
    n_row, n_pitch, n_span = sizes
    half = NK // n_pitch // 2
    vmem, dma = pltpu.VMEM, pltpu.SemaphoreType.DMA
    anywhere = pl.BlockSpec(memory_space=pl.ANY)
    scalars = pl.BlockSpec(memory_space=pltpu.SMEM)
    updated, wall = pl.pallas_call(
        functools.partial(section, sizes),
        out_shape=(
            jax.ShapeDtypeStruct((ROWS, NS), F32),
            jax.ShapeDtypeStruct((TC, NK // NS, NS), F32),
        ),
        in_specs=[scalars] * 4 + [anywhere] * 4,
        out_specs=(anywhere, pl.BlockSpec(memory_space=pltpu.VMEM)),
        scratch_shapes=[
            vmem((ROWS, NS), F32),
            vmem((ROWS, NS), F32),
            vmem((NT * NJ, NC * NS), F32),
            vmem((n_row, H * NC, 2, NS), F32),
            vmem((PAD, NC * NS), F32),
            vmem((4 * PAD, NC * NS), BF16),
            vmem((NT * NJ, 2 * NS), BF16),
            vmem((1, NK), I32),
            vmem((1, NK), I32),
            vmem((2 * NS, NK), BF16),
            vmem((NJ, NK), F32),
            vmem((2 * NS, NK), BF16),
            vmem((NK, NK), BF16),
            vmem((PAD, 2 * NS), BF16),
            vmem((PAD, 2 * NS), BF16),
            vmem((2, 2, PAD, NS), F32),
            vmem((2, 2, PAD, NS), F32),
            vmem((2, PAD // 2, NS), F32),
            vmem((2, PAD // 2, NS), F32),
            vmem((PAD, NS), F32),
            vmem((5, PAD, NS), F32),
            vmem((NT, NC, NK), F32),
            vmem((PAD, NK), F32),
            vmem((NK, NS), F32),
            vmem((n_pitch, half, NS), F32),
            vmem((n_pitch, half, NS), F32),
            dma((3,)),
            dma((2,)),
            dma((2,)),
            dma((2,)),
            dma((2,)),
            dma((n_row,)),
            dma,
            dma,
            dma,
            dma,
        ],
        compiler_params=pltpu.CompilerParams(
            collective_id=1, has_side_effects=True, vmem_limit_bytes=32 * 1024 * 1024
        ),
        name="flux_section",
    )(
        blades,
        harmonics,
        pitch_jac,
        span_jac,
        unknowns.reshape(ROWS, NS),
        jnp.transpose(spectrum[0], (1, 2, 0, 3)).reshape(H * NC, 2, NS),
        send_cell.reshape(1, NK),
        recv_order.reshape(1, NK),
    )
    return (
        updated.reshape(unknowns.shape),
        wall.reshape(1, 1, NT, NC, NK),
    )


def solution(mesh):
    sizes = (mesh.shape["row"], mesh.shape["pitch"], mesh.shape["span"])
    return jax.shard_map(
        functools.partial(local, sizes),
        mesh=mesh,
        in_specs=(
            P("row", None, None, "pitch", "span"),
            P("row", None, None, None, "span"),
            P(),
            P(),
            P(),
            P(),
            P("row", "span", "pitch", None),
            P("row", "span", "pitch", None),
        ),
        out_specs=(P("row", None, None, "pitch", "span"), P("row", "span", None, None, "pitch")),
        check_vma=False,
    )
```

```python
import functools
import math

import jax
import jax.numpy as jnp
import numpy as np
from jax import lax
from jax.experimental import pallas as pl
from jax.experimental.pallas import tpu as pltpu
from jax.sharding import PartitionSpec as P

MESH = pl.DeviceIdType.MESH
F32, BF16, I32 = jnp.float32, jnp.bfloat16, jnp.int32

H = 5
NT = 11
NC = 5
NJ = 32
NS = 128
NK = 256
TC = NT * NC
PAD = 64
ROWS = TC * NJ
PARTS = 5

step_size = 0.25
damping = 1.0 / 16.0
coupling = 0.5
frequency = 0.5
far_weight = 0.5

d_entries = [
    float(np.float32(0.5 * frequency * math.cos(math.pi * n) / math.sin(math.pi * n / NT)))
    for n in range(1, NT // 2 + 1)
]


def iota(shape, dim):
    return lax.broadcasted_iota(I32, shape, dim)


def split(x):
    high = x.astype(BF16)
    return high, (x - high.astype(F32)).astype(BF16)


def dot(a, b):
    return lax.dot_general(a, b, (((1,), (0,)), ((), ())), preferred_element_type=F32)


def one_hot(condition):
    return jnp.where(condition, 1.0, 0.0).astype(BF16)


def section(
    sizes,
    blades_hbm,
    harmonics_hbm,
    pitch_jac_hbm,
    span_jac_hbm,
    u_hbm,
    spec_hbm,
    cell_hbm,
    upd_ref,
    arrived,
    blades,
    harmonics,
    pitch_jac,
    span_jac,
    u_ref,
    heard_ref,
    specs,
    coeff_ref,
    rhs_ref,
    table_ref,
    cell_ref,
    cell_s,
    cell_j,
    cell_edge,
    mix_p,
    mix_s,
    pitch_out,
    pitch_in,
    span_out,
    span_in,
    edge_ref,
    corr_ref,
    g_part,
    g_ref,
    turn_ref,
    outgoing,
    load_sem,
    pitch_send,
    pitch_recv,
    span_send,
    span_recv,
    row_send,
    row_recv,
    wall_send,
    wall_recv,
):
    n_row, n_pitch, n_span = sizes
    handoff = NK // n_pitch
    half = handoff // 2
    r, p, s = lax.axis_index("row"), lax.axis_index("pitch"), lax.axis_index("span")

    def pitch_peer(k):
        return (r, lax.rem(p + k, n_pitch), s)

    def row_peer(k):
        return (lax.rem(r + k, n_row), p, s)

    barrier = pltpu.get_barrier_semaphore()
    span_ring = (1, n_span - 1) if n_span > 2 else (1,)
    for k in span_ring:
        pl.semaphore_signal(
            barrier, inc=1, device_id=(r, p, lax.rem(s + k, n_span)), device_id_type=MESH
        )
    for k in (1, n_pitch - 1):
        pl.semaphore_signal(barrier, inc=1, device_id=pitch_peer(k), device_id_type=MESH)
    for k in range(1, n_row):
        pl.semaphore_signal(barrier, inc=1, device_id=row_peer(k), device_id_type=MESH)

    def greet(k, carry):
        pl.semaphore_signal(barrier, inc=1, device_id=pitch_peer(k), device_id_type=MESH)
        return carry

    lax.fori_loop(2, n_pitch - 1, greet, 0)

    load_u = pltpu.make_async_copy(u_hbm, u_ref, load_sem.at[0])
    load_cell = pltpu.make_async_copy(cell_hbm, cell_ref, load_sem.at[1])
    load_u.start()
    load_cell.start()
    scalars = []
    for i, (src, dst) in enumerate(
        (
            (blades_hbm, blades),
            (harmonics_hbm, harmonics),
            (pitch_jac_hbm, pitch_jac),
            (span_jac_hbm, span_jac),
        )
    ):
        copy = pltpu.make_async_copy(src, dst, load_sem.at[2 + i])
        copy.start()
        scalars.append(copy)

    lane = iota((1, NS), 1)

    pitch_out[...] = jnp.zeros_like(pitch_out)
    edge_ref[...] = jnp.zeros_like(edge_ref)
    g_ref[...] = jnp.zeros_like(g_ref)
    coeff_ref[...] = jnp.zeros_like(coeff_ref)

    @pl.when(s == 0)
    def _():
        span_in[0] = jnp.zeros_like(span_in[0])

    @pl.when(s == n_span - 1)
    def _():
        span_in[1] = jnp.zeros_like(span_in[1])

    load_u.wait()
    for layer in range(2):
        pitch_out[0, layer, 0:TC, :] = u_ref[pl.ds(NJ - 2 + layer, TC, stride=NJ), :]
        pitch_out[1, layer, 0:TC, :] = u_ref[pl.ds(layer, TC, stride=NJ), :]
    edges = jnp.zeros((TC, NS), F32)
    for j in range(NJ):
        turned = pltpu.roll(u_ref[pl.ds(j, TC, stride=NJ), :], (2 + 4 * j) % NS, 1)
        edges = jnp.where((lane >= 4 * j) & (lane < 4 * j + 4), turned, edges)
    edge_ref[0:TC, :] = edges
    e4 = lax.rem(lane, 4)
    low, high = edge_ref[0 : PAD // 2, :], edge_ref[PAD // 2 : PAD, :]
    span_out[0] = jnp.where(e4 < 2, low, pltpu.roll(high, 2, 1))
    span_out[1] = jnp.where(e4 >= 2, low, pltpu.roll(high, NS - 2, 1))

    pl.semaphore_wait(barrier, len(span_ring) + n_row - 1 + n_pitch - 1)
    right = pltpu.make_async_remote_copy(
        span_out.at[0],
        span_in.at[0],
        span_send.at[0],
        span_recv.at[0],
        device_id=(r, p, lax.rem(s + 1, n_span)),
        device_id_type=MESH,
    )
    left = pltpu.make_async_remote_copy(
        span_out.at[1],
        span_in.at[1],
        span_send.at[1],
        span_recv.at[1],
        device_id=(r, p, lax.rem(s + n_span - 1, n_span)),
        device_id_type=MESH,
    )

    @pl.when(s < n_span - 1)
    def _():
        right.start()

    @pl.when(s > 0)
    def _():
        left.start()

    halos = []
    for way, k in ((0, 1), (1, n_pitch - 1)):
        copy = pltpu.make_async_remote_copy(
            pitch_out.at[way],
            pitch_in.at[way],
            pitch_send.at[way],
            pitch_recv.at[way],
            device_id=pitch_peer(k),
            device_id_type=MESH,
        )
        copy.start()
        halos.append(copy)
    spectra = []
    for k in range(1, n_row):
        copy = pltpu.make_async_remote_copy(
            spec_hbm,
            specs.at[r],
            row_send.at[k],
            row_recv,
            device_id=row_peer(k),
            device_id_type=MESH,
        )
        copy.start()
        spectra.append(copy)
    pltpu.make_async_copy(spec_hbm, specs.at[r], row_recv).start()

    load_cell.wait()
    for copy in scalars:
        copy.wait()
    cell = cell_ref[...]
    cj, cs = cell // NS, lax.rem(cell, NS)
    cell_s[...] = one_hot((iota((2 * NS, NK), 0) & (NS - 1)) == cs)
    cell_j[...] = jnp.where(iota((NJ, NK), 0) == cj, 1.0, 0.0)
    place = iota((2 * NS, NK), 0) & (NS - 1)
    e_row = place & 3
    column = jnp.where(e_row < 2, e_row, NS - 4 + e_row)
    cell_edge[...] = one_hot((place // 4 == cj) & (column == cs))

    mr, mc = iota((PAD, NS), 0), iota((PAD, NS), 1) & (PAD - 1)
    tr, tcol = (mr * 205) >> 10, (mc * 205) >> 10
    cr, cc = mr - 5 * tr, mc - 5 * tcol
    same = (tr == tcol) & (mr < TC) & (mc < TC)
    pair = jnp.where(same, cr * NC + cc, -1)
    for jac, mix in ((pitch_jac, mix_p), (span_jac, mix_s)):
        m = jnp.zeros((PAD, NS), F32)
        for a in range(NC):
            for c in range(NC):
                m = jnp.where(pair == a * NC + c, jac[a, c], m)
        mh, ml = split(m)
        mix[:, 0:NS] = mh
        mix[:, NS : 2 * NS] = ml

    l64 = lane & (PAD - 1)
    lg, lk = l64 // 16, l64 & 15
    order_of = jnp.zeros((1, NS), I32)
    turns_of = jnp.zeros((1, NS), I32)
    weight = jnp.zeros((1, NS), F32)
    for g in range(n_row):
        distance = jnp.abs(r - g)
        w = jnp.where(distance == 1, 1.0, jnp.where(distance >= 2, far_weight, 0.0)).astype(F32)
        weight = jnp.where((lg == g) & (lk < 2 * H), w, weight)
        for n in range(H):
            here = (lg == g) & (lk // 2 == n)
            order_of = jnp.where(here, harmonics[g, n], order_of)
            turns_of = jnp.where(here, harmonics[g, n] * blades[g], turns_of)
    whole = n_pitch * NJ
    cells = p * NJ + iota((NJ, NS), 0)
    phase_j = ((turns_of * cells) & (whole - 1)).astype(F32) * (2.0 * math.pi / whole)
    phase_j = phase_j - (lk & 1).astype(F32) * (0.5 * math.pi)
    times = order_of * iota((16, NS), 0)
    times = times - NT * ((times * 5958) >> 16)
    phase_t = times.astype(F32) * (2.0 * math.pi / NT)
    cos_j, sin_j = weight * jnp.cos(phase_j), weight * jnp.sin(phase_j)
    cos_t, sin_t = jnp.cos(phase_t), jnp.sin(phase_t)
    for t in range(NT):
        high, low = split(cos_t[t : t + 1] * cos_j - sin_t[t : t + 1] * sin_j)
        table_ref[t * NJ : (t + 1) * NJ, 0:NS] = high
        table_ref[t * NJ : (t + 1) * NJ, NS : 2 * NS] = low

    row = iota((1, NJ, 1), 1)

    def at(t):
        return pl.ds(pl.multiple_of(t * (NC * NJ), NC * NJ), NC * NJ)

    def interior(t, carry):
        x = u_ref[at(t), :]
        m1 = jnp.where(lane >= 1, pltpu.roll(x, 1, 1), 0.0)
        m2 = jnp.where(lane >= 2, pltpu.roll(x, 2, 1), 0.0)
        p1 = jnp.where(lane < NS - 1, pltpu.roll(x, NS - 1, 1), 0.0)
        p2 = jnp.where(lane < NS - 2, pltpu.roll(x, NS - 2, 1), 0.0)
        d1s = (0.5 * (p1 - m1)).reshape(NC, NJ, NS)
        fourth = ((p2 + m2) - 4.0 * (p1 + m1)).reshape(NC, NJ, NS)
        x = x.reshape(NC, NJ, NS)
        m1 = jnp.where(row >= 1, pltpu.roll(x, 1, 1), 0.0)
        m2 = jnp.where(row >= 2, pltpu.roll(x, 2, 1), 0.0)
        p1 = jnp.where(row < NJ - 1, pltpu.roll(x, NJ - 1, 1), 0.0)
        p2 = jnp.where(row < NJ - 2, pltpu.roll(x, NJ - 2, 1), 0.0)
        d1p = 0.5 * (p1 - m1)
        fourth = fourth + ((p2 + m2) - 4.0 * (p1 + m1))
        change = damping * fourth + (12.0 * damping + 2.0 * coupling) * x
        for n in range(1, NT // 2 + 1):
            before = u_ref[at(lax.rem(t + NT - n, NT)), :]
            after = u_ref[at(lax.rem(t + n, NT)), :]
            change = change + d_entries[n - 1] * (before - after).reshape(NC, NJ, NS)
        for a in range(NC):
            flux = change[a]
            for c in range(NC):
                flux = flux + pitch_jac[a, c] * d1p[c] + span_jac[a, c] * d1s[c]
            upd_ref[pl.ds(pl.multiple_of((t * NC + a) * NJ, NJ), NJ), :] = x[a] - step_size * flux
        return carry

    lax.fori_loop(0, NT, interior, 0)

    pltpu.make_async_copy(specs, specs, row_recv).wait()
    for g in range(n_row):
        for n in range(H):
            for c in range(NC):
                coeff_ref[16 * g + 2 * n : 16 * g + 2 * n + 2, c * NS : (c + 1) * NS] = specs[
                    g, n * NC + c
                ]
    high, low = split(coeff_ref[...])
    for k in range(2):
        rhs_ref[2 * PAD * k : 2 * PAD * k + PAD, :] = high
        rhs_ref[2 * PAD * k + PAD : 2 * PAD * (k + 1), :] = low
    heard_ref[...] = dot(table_ref[...], rhs_ref[...])

    def gather(t, carry):
        heard = heard_ref[pl.ds(pl.multiple_of(t * NJ, NJ), NJ), :]
        heard = jnp.concatenate([heard[:, c * NS : (c + 1) * NS] for c in range(NC)], axis=0)
        x = upd_ref[at(t), :] + (step_size * coupling) * heard
        upd_ref[at(t), :] = x
        high, low = split(x)
        found = dot(jnp.concatenate([high, low], axis=1), cell_s[...])
        found = found.reshape(NC, NJ, NK) * cell_j[...]
        g_part[t] = jnp.sum(found, axis=1)
        return carry

    lax.fori_loop(0, NT, gather, 0)
    for t in range(NT):
        g_ref[t * NC : (t + 1) * NC, :] = g_part[t]

    @pl.when(s < n_span - 1)
    def _():
        left_in = pltpu.make_async_copy(span_in.at[1], span_in.at[1], span_recv.at[1])
        left_in.wait()

    @pl.when(s > 0)
    def _():
        right_in = pltpu.make_async_copy(span_in.at[0], span_in.at[0], span_recv.at[0])
        right_in.wait()

    from_left, from_right = span_in[0], span_in[1]
    x = jnp.concatenate(
        [
            jnp.where(e4 < 2, from_left, from_right),
            jnp.where(e4 < 2, pltpu.roll(from_left, NS - 2, 1), pltpu.roll(from_right, 2, 1)),
        ],
        axis=0,
    )
    y = jnp.where(e4 == 0, pltpu.roll(x, NS - 1, 1), jnp.where(e4 == 3, pltpu.roll(x, 1, 1), 0.0))
    sign = jnp.where(e4 == 0, -0.5, jnp.where(e4 == 3, 0.5, 0.0))
    high, low = split(y)
    mixed = dot(mix_s[...], jnp.concatenate([high, low, high, low], axis=0))
    corr_ref[4] = -step_size * (sign * mixed + damping * (x - 4.0 * y))

    for copy in halos:
        copy.wait_recv()
    inner = jnp.concatenate([pitch_in[0, 1], pitch_in[1, 0]], axis=1)
    high, low = split(inner)
    mixed = dot(mix_p[...], jnp.concatenate([high, low, high, low], axis=0))
    corr_ref[0] = -step_size * (
        -0.5 * mixed[:, 0:NS] + damping * (pitch_in[0, 0] - 4.0 * pitch_in[0, 1])
    )
    corr_ref[1] = (-step_size * damping) * pitch_in[0, 1]
    corr_ref[2] = (-step_size * damping) * pitch_in[1, 0]
    corr_ref[3] = -step_size * (
        0.5 * mixed[:, NS : 2 * NS] + damping * (pitch_in[1, 1] - 4.0 * pitch_in[1, 0])
    )

    high, low = split(corr_ref[4])
    total = g_ref[...] + dot(jnp.concatenate([high, low], axis=1), cell_edge[...])
    high, low = split(corr_ref[0:4].reshape(4 * PAD, NS))
    found = dot(jnp.concatenate([high, low], axis=1), cell_s[...])
    for e, at_row in enumerate((0, 1, NJ - 2, NJ - 1)):
        total = total + found[e * PAD : (e + 1) * PAD] * cell_j[at_row : at_row + 1, :]

    turn_ref[...] = jnp.concatenate([total, pltpu.roll(total, NK - 1, 1)], axis=0).T
    for i in range(half):
        outgoing[:, i, :] = turn_ref[pl.ds(2 * i, n_pitch, stride=handoff), :]

    def send(k, carry):
        q = lax.rem(p + k, n_pitch)
        pltpu.make_async_remote_copy(
            outgoing.at[q],
            arrived.at[p],
            wall_send,
            wall_recv,
            device_id=(r, q, s),
            device_id_type=MESH,
        ).start()
        return carry

    lax.fori_loop(1, n_pitch, send, 0)
    pltpu.make_async_copy(outgoing.at[p], arrived.at[p], wall_recv).start()

    for e, at_row in enumerate((0, 1, NJ - 2, NJ - 1)):
        rows = pl.ds(at_row, TC, stride=NJ)
        upd_ref[rows, :] = upd_ref[rows, :] + corr_ref[e, 0:TC, :]
    e_lane = iota((2 * NS, NS), 0) & 3
    to_column = one_hot(iota((2 * NS, NS), 1) == jnp.where(e_lane < 2, e_lane, NS - 4 + e_lane))
    own = lane // 4 == iota((NJ, NS), 0)
    for t in range(NT):
        spread = jnp.concatenate(
            [
                jnp.where(own, corr_ref[4, t * NC + c : t * NC + c + 1, :], 0.0)
                for c in range(NC)
            ],
            axis=0,
        )
        high, low = split(spread)
        rows = slice(t * NC * NJ, (t + 1) * NC * NJ)
        upd_ref[rows, :] = upd_ref[rows, :] + dot(
            jnp.concatenate([high, low], axis=1), to_column
        )

    pltpu.make_async_copy(arrived, arrived, wall_recv).wait()
    some = outgoing.at[pl.ds(0, n_pitch - 1)]
    pltpu.make_async_copy(some, some, wall_send).wait()
    for copy in halos + spectra:
        copy.wait_send()

    @pl.when(s < n_span - 1)
    def _():
        right.wait_send()

    @pl.when(s > 0)
    def _():
        left.wait_send()


def finish(sizes, upd_ref, arrived, order_hbm, out_hbm, wall_ref, order_ref, sem):
    n_pitch = sizes[1]
    handoff = NK // n_pitch
    load = pltpu.make_async_copy(order_hbm, order_ref, sem.at[0])
    load.start()
    stores = []
    for i in range(PARTS):
        part = pl.ds(i * (ROWS // PARTS), ROWS // PARTS)
        copy = pltpu.make_async_copy(upd_ref.at[part], out_hbm.at[part], sem.at[1 + i])
        copy.start()
        stores.append(copy)
    load.wait()

    slots = jnp.concatenate([arrived[:, i, :] for i in range(handoff // 2)], axis=0).T
    high, low = split(jnp.concatenate([slots[0:PAD], slots[PAD : 2 * PAD]], axis=1))
    rho = iota((NK, NK), 0)
    rest = rho & (NS - 1)
    slot = (rest & (n_pitch - 1)) * handoff + (rest // n_pitch) * 2 + rho // NS
    placed = dot(jnp.concatenate([high, low], axis=0), one_hot(slot == order_ref[...]))
    placed = placed[0:PAD] + placed[PAD : 2 * PAD]
    for k in range(NK // NS):
        wall_ref[:, k, :] = placed[0:TC, k * NS : (k + 1) * NS]
    for copy in stores:
        copy.wait()


def local(sizes, unknowns, spectrum, blades, harmonics, pitch_jac, span_jac, send_cell, recv_order):
    n_row, n_pitch, n_span = sizes
    half = NK // n_pitch // 2
    vmem, dma = pltpu.VMEM, pltpu.SemaphoreType.DMA
    in_hbm = pl.BlockSpec(memory_space=pltpu.HBM)
    in_vmem = pl.BlockSpec(memory_space=pltpu.VMEM)
    smem = pltpu.SMEM
    updated, arrived = pl.pallas_call(
        functools.partial(section, sizes),
        out_shape=(vmem((ROWS, NS), F32), vmem((n_pitch, half, NS), F32)),
        in_specs=[in_hbm] * 7,
        out_specs=(in_vmem, in_vmem),
        scratch_shapes=[
            smem((n_row,), I32),
            smem((n_row, H), I32),
            smem((NC, NC), F32),
            smem((NC, NC), F32),
            vmem((ROWS, NS), F32),
            vmem((NT * NJ, NC * NS), F32),
            vmem((n_row, H * NC, 2, NS), F32),
            vmem((PAD, NC * NS), F32),
            vmem((4 * PAD, NC * NS), BF16),
            vmem((NT * NJ, 2 * NS), BF16),
            vmem((1, NK), I32),
            vmem((2 * NS, NK), BF16),
            vmem((NJ, NK), F32),
            vmem((2 * NS, NK), BF16),
            vmem((PAD, 2 * NS), BF16),
            vmem((PAD, 2 * NS), BF16),
            vmem((2, 2, PAD, NS), F32),
            vmem((2, 2, PAD, NS), F32),
            vmem((2, PAD // 2, NS), F32),
            vmem((2, PAD // 2, NS), F32),
            vmem((PAD, NS), F32),
            vmem((5, PAD, NS), F32),
            vmem((NT, NC, NK), F32),
            vmem((PAD, NK), F32),
            vmem((NK, NS), F32),
            vmem((n_pitch, half, NS), F32),
            dma((6,)),
            dma((2,)),
            dma((2,)),
            dma((2,)),
            dma((2,)),
            dma((n_row,)),
            dma,
            dma,
            dma,
        ],
        compiler_params=pltpu.CompilerParams(
            collective_id=1, has_side_effects=True, vmem_limit_bytes=32 * 1024 * 1024
        ),
        name="flux_section",
    )(
        *(
            pltpu.with_memory_space_constraint(x, pltpu.HBM)
            for x in (
                blades,
                harmonics,
                pitch_jac,
                span_jac,
                unknowns.reshape(ROWS, NS),
                jnp.transpose(spectrum[0], (1, 2, 0, 3)).reshape(H * NC, 2, NS),
                send_cell.reshape(1, NK),
            )
        )
    )
    updated, wall = pl.pallas_call(
        functools.partial(finish, sizes),
        out_shape=(
            jax.ShapeDtypeStruct((ROWS, NS), F32),
            jax.ShapeDtypeStruct((TC, NK // NS, NS), F32),
        ),
        in_specs=[in_vmem, in_vmem, in_hbm],
        out_specs=(in_hbm, in_vmem),
        scratch_shapes=[
            vmem((1, NK), I32),
            dma((1 + PARTS,)),
        ],
        compiler_params=pltpu.CompilerParams(vmem_limit_bytes=8 * 1024 * 1024),
        name="wall_order",
    )(
        updated,
        arrived,
        pltpu.with_memory_space_constraint(recv_order.reshape(1, NK), pltpu.HBM),
    )
    return (
        updated.reshape(unknowns.shape),
        wall.reshape(1, 1, NT, NC, NK),
    )


def solution(mesh):
    sizes = (mesh.shape["row"], mesh.shape["pitch"], mesh.shape["span"])
    return jax.shard_map(
        functools.partial(local, sizes),
        mesh=mesh,
        in_specs=(
            P("row", None, None, "pitch", "span"),
            P("row", None, None, None, "span"),
            P(),
            P(),
            P(),
            P(),
            P("row", "span", "pitch", None),
            P("row", "span", "pitch", None),
        ),
        out_specs=(P("row", None, None, "pitch", "span"), P("row", "span", None, None, "pitch")),
        check_vma=False,
    )
```

```python
import functools
import math

import jax
import jax.numpy as jnp
import numpy as np
from jax import lax
from jax.experimental import pallas as pl
from jax.experimental.pallas import tpu as pltpu
from jax.sharding import PartitionSpec as P

MESH = pl.DeviceIdType.MESH
F32, BF16, I32 = jnp.float32, jnp.bfloat16, jnp.int32

H = 5
NT = 11
NC = 5
NJ = 32
NS = 128
NK = 256
TC = NT * NC
PAD = 64
ROWS = TC * NJ
PARTS = 5

step_size = 0.25
damping = 1.0 / 16.0
coupling = 0.5
frequency = 0.5
far_weight = 0.5

d_entries = [
    float(np.float32(0.5 * frequency * math.cos(math.pi * n) / math.sin(math.pi * n / NT)))
    for n in range(1, NT // 2 + 1)
]


def iota(shape, dim):
    return lax.broadcasted_iota(I32, shape, dim)


def split(x):
    high = x.astype(BF16)
    return high, (x - high.astype(F32)).astype(BF16)


def dot(a, b):
    return lax.dot_general(a, b, (((1,), (0,)), ((), ())), preferred_element_type=F32)


def one_hot(condition):
    return jnp.where(condition, 1.0, 0.0).astype(BF16)


def section(
    sizes,
    blades_hbm,
    harmonics_hbm,
    pitch_jac_hbm,
    span_jac_hbm,
    u_hbm,
    spec_hbm,
    cell_hbm,
    order_hbm,
    upd_ref,
    arrived,
    slot_ref,
    blades,
    harmonics,
    pitch_jac,
    span_jac,
    u_ref,
    heard_ref,
    specs,
    coeff_ref,
    rhs_ref,
    table_ref,
    cell_ref,
    order_ref,
    cell_s,
    cell_j,
    cell_edge,
    mix_p,
    mix_s,
    pitch_out,
    pitch_in,
    span_out,
    span_in,
    edge_ref,
    corr_ref,
    g_part,
    g_ref,
    turn_ref,
    outgoing,
    load_sem,
    pitch_send,
    pitch_recv,
    span_send,
    span_recv,
    row_send,
    row_recv,
    wall_send,
    wall_recv,
    answer,
):
    n_row, n_pitch, n_span = sizes
    handoff = NK // n_pitch
    half = handoff // 2
    r, p, s = lax.axis_index("row"), lax.axis_index("pitch"), lax.axis_index("span")

    def pitch_peer(k):
        return (r, lax.rem(p + k, n_pitch), s)

    def row_peer(k):
        return (lax.rem(r + k, n_row), p, s)

    loads = []
    for i in range(PARTS):
        part = pl.ds(i * (ROWS // PARTS), ROWS // PARTS)
        copy = pltpu.make_async_copy(u_hbm.at[part], u_ref.at[part], load_sem.at[i])
        copy.start()
        loads.append(copy)

    middle = n_span // 2
    mate = s + 1 - 2 * lax.rem(s, 2)
    below, above = s == middle - 1, s == middle

    def span_peer(k):
        return (r, p, lax.rem(s + k + n_span, n_span))

    barrier = pltpu.get_barrier_semaphore()
    pl.semaphore_signal(barrier, inc=1, device_id=(r, p, mate), device_id_type=MESH)

    @pl.when(below)
    def _():
        pl.semaphore_signal(barrier, inc=1, device_id=span_peer(1), device_id_type=MESH)

    for k in (1, n_pitch - 1):
        pl.semaphore_signal(barrier, inc=1, device_id=pitch_peer(k), device_id_type=MESH)
    for k in range(1, n_row):
        pl.semaphore_signal(barrier, inc=1, device_id=row_peer(k), device_id_type=MESH)

    def greet(k, carry):
        pl.semaphore_signal(barrier, inc=1, device_id=pitch_peer(k), device_id_type=MESH)
        return carry

    lax.fori_loop(2, n_pitch - 1, greet, 0)

    scalars = []
    for i, (src, dst) in enumerate(
        (
            (blades_hbm, blades),
            (harmonics_hbm, harmonics),
            (pitch_jac_hbm, pitch_jac),
            (span_jac_hbm, span_jac),
            (cell_hbm, cell_ref),
            (order_hbm, order_ref),
        )
    ):
        copy = pltpu.make_async_copy(src, dst, load_sem.at[PARTS + i])
        copy.start()
        scalars.append(copy)

    lane = iota((1, NS), 1)

    for copy in loads:
        copy.wait()
    edges = jnp.zeros((TC, NS), F32)
    for j in range(NJ):
        turned = pltpu.roll(u_ref[pl.ds(j, TC, stride=NJ), :], (2 + 4 * j) % NS, 1)
        edges = jnp.where((lane >= 4 * j) & (lane < 4 * j + 4), turned, edges)
    edge_ref[0:TC, :] = edges
    edge_ref[TC:PAD, :] = jnp.zeros((PAD - TC, NS), F32)
    e4 = lax.rem(lane, 4)
    low, high = edge_ref[0 : PAD // 2, :], edge_ref[PAD // 2 : PAD, :]
    span_out[0] = jnp.where(e4 < 2, low, pltpu.roll(high, 2, 1))
    span_out[1] = jnp.where(e4 >= 2, low, pltpu.roll(high, NS - 2, 1))

    greeters = 1 + n_row - 1 + n_pitch - 1
    pl.semaphore_wait(barrier, jnp.where(above, greeters + 1, greeters))

    @pl.when(above)
    def _():
        pl.semaphore_signal(answer, inc=1, device_id=span_peer(-1), device_id_type=MESH)

    right = pltpu.make_async_remote_copy(
        span_out.at[0],
        span_in.at[0],
        span_send.at[0],
        span_recv.at[0],
        device_id=span_peer(1),
        device_id_type=MESH,
    )
    left = pltpu.make_async_remote_copy(
        span_out.at[1],
        span_in.at[1],
        span_send.at[1],
        span_recv.at[1],
        device_id=span_peer(-1),
        device_id_type=MESH,
    )

    @pl.when(s > 0)
    def _():
        left.start()

    @pl.when((s < n_span - 1) & (s != middle - 1))
    def _():
        right.start()

    pitch_out[:, :, TC:PAD, :] = jnp.zeros((2, 2, PAD - TC, NS), F32)
    for layer in range(2):
        pitch_out[0, layer, 0:TC, :] = u_ref[pl.ds(NJ - 2 + layer, TC, stride=NJ), :]
        pitch_out[1, layer, 0:TC, :] = u_ref[pl.ds(layer, TC, stride=NJ), :]

    halos = []
    for way, k in ((0, 1), (1, n_pitch - 1)):
        copy = pltpu.make_async_remote_copy(
            pitch_out.at[way],
            pitch_in.at[way],
            pitch_send.at[way],
            pitch_recv.at[way],
            device_id=pitch_peer(k),
            device_id_type=MESH,
        )
        copy.start()
        halos.append(copy)
    spectra = []
    for k in range(1, n_row):
        copy = pltpu.make_async_remote_copy(
            spec_hbm,
            specs.at[r],
            row_send.at[k],
            row_recv,
            device_id=row_peer(k),
            device_id_type=MESH,
        )
        copy.start()
        spectra.append(copy)
    pltpu.make_async_copy(spec_hbm, specs.at[r], row_recv).start()

    g_ref[TC:PAD, :] = jnp.zeros((PAD - TC, NK), F32)
    coeff_ref[...] = jnp.zeros_like(coeff_ref)

    @pl.when(s == 0)
    def _():
        span_in[0] = jnp.zeros_like(span_in[0])

    @pl.when(s == n_span - 1)
    def _():
        span_in[1] = jnp.zeros_like(span_in[1])

    for copy in scalars:
        copy.wait()
    cell = cell_ref[...]
    cj, cs = cell // NS, lax.rem(cell, NS)
    cell_s[...] = one_hot((iota((2 * NS, NK), 0) & (NS - 1)) == cs)
    cell_j[...] = jnp.where(iota((NJ, NK), 0) == cj, 1.0, 0.0)
    place = iota((2 * NS, NK), 0) & (NS - 1)
    e_row = place & 3
    column = jnp.where(e_row < 2, e_row, NS - 4 + e_row)
    cell_edge[...] = one_hot((place // 4 == cj) & (column == cs))
    rho = iota((NK, NK), 0)
    rest = rho & (NS - 1)
    slot = (rest & (n_pitch - 1)) * handoff + (rest // n_pitch) * 2 + rho // NS
    slot_ref[...] = one_hot(slot == order_ref[...])

    mr, mc = iota((PAD, NS), 0), iota((PAD, NS), 1) & (PAD - 1)
    tr, tcol = (mr * 205) >> 10, (mc * 205) >> 10
    cr, cc = mr - 5 * tr, mc - 5 * tcol
    same = (tr == tcol) & (mr < TC) & (mc < TC)
    pair = jnp.where(same, cr * NC + cc, -1)
    for jac, mix in ((pitch_jac, mix_p), (span_jac, mix_s)):
        m = jnp.zeros((PAD, NS), F32)
        for a in range(NC):
            for c in range(NC):
                m = jnp.where(pair == a * NC + c, jac[a, c], m)
        mh, ml = split(m)
        mix[:, 0:NS] = mh
        mix[:, NS : 2 * NS] = ml

    l64 = lane & (PAD - 1)
    lg, lk = l64 // 16, l64 & 15
    order_of = jnp.zeros((1, NS), I32)
    turns_of = jnp.zeros((1, NS), I32)
    weight = jnp.zeros((1, NS), F32)
    for g in range(n_row):
        distance = jnp.abs(r - g)
        w = jnp.where(distance == 1, 1.0, jnp.where(distance >= 2, far_weight, 0.0)).astype(F32)
        weight = jnp.where((lg == g) & (lk < 2 * H), w, weight)
        for n in range(H):
            here = (lg == g) & (lk // 2 == n)
            order_of = jnp.where(here, harmonics[g, n], order_of)
            turns_of = jnp.where(here, harmonics[g, n] * blades[g], turns_of)
    whole = n_pitch * NJ
    cells = p * NJ + iota((NJ, NS), 0)
    phase_j = ((turns_of * cells) & (whole - 1)).astype(F32) * (2.0 * math.pi / whole)
    phase_j = phase_j - (lk & 1).astype(F32) * (0.5 * math.pi)
    times = order_of * iota((16, NS), 0)
    times = times - NT * ((times * 5958) >> 16)
    phase_t = times.astype(F32) * (2.0 * math.pi / NT)
    cos_j, sin_j = weight * jnp.cos(phase_j), weight * jnp.sin(phase_j)
    cos_t, sin_t = jnp.cos(phase_t), jnp.sin(phase_t)
    for t in range(NT):
        high, low = split(cos_t[t : t + 1] * cos_j - sin_t[t : t + 1] * sin_j)
        table_ref[t * NJ : (t + 1) * NJ, 0:NS] = high
        table_ref[t * NJ : (t + 1) * NJ, NS : 2 * NS] = low

    row = iota((1, NJ, 1), 1)

    def at(t):
        return pl.ds(pl.multiple_of(t * (NC * NJ), NC * NJ), NC * NJ)

    def interior(t, carry):
        x = u_ref[at(t), :]
        m1 = jnp.where(lane >= 1, pltpu.roll(x, 1, 1), 0.0)
        m2 = jnp.where(lane >= 2, pltpu.roll(x, 2, 1), 0.0)
        p1 = jnp.where(lane < NS - 1, pltpu.roll(x, NS - 1, 1), 0.0)
        p2 = jnp.where(lane < NS - 2, pltpu.roll(x, NS - 2, 1), 0.0)
        d1s = (0.5 * (p1 - m1)).reshape(NC, NJ, NS)
        fourth = ((p2 + m2) - 4.0 * (p1 + m1)).reshape(NC, NJ, NS)
        x = x.reshape(NC, NJ, NS)
        m1 = jnp.where(row >= 1, pltpu.roll(x, 1, 1), 0.0)
        m2 = jnp.where(row >= 2, pltpu.roll(x, 2, 1), 0.0)
        p1 = jnp.where(row < NJ - 1, pltpu.roll(x, NJ - 1, 1), 0.0)
        p2 = jnp.where(row < NJ - 2, pltpu.roll(x, NJ - 2, 1), 0.0)
        d1p = 0.5 * (p1 - m1)
        fourth = fourth + ((p2 + m2) - 4.0 * (p1 + m1))
        change = damping * fourth + (12.0 * damping + 2.0 * coupling) * x
        for n in range(1, NT // 2 + 1):
            before = u_ref[at(lax.rem(t + NT - n, NT)), :]
            after = u_ref[at(lax.rem(t + n, NT)), :]
            change = change + d_entries[n - 1] * (before - after).reshape(NC, NJ, NS)
        for a in range(NC):
            flux = change[a]
            for c in range(NC):
                flux = flux + pitch_jac[a, c] * d1p[c] + span_jac[a, c] * d1s[c]
            upd_ref[pl.ds(pl.multiple_of((t * NC + a) * NJ, NJ), NJ), :] = x[a] - step_size * flux
        return carry

    lax.fori_loop(0, NT, interior, 0)

    pltpu.make_async_copy(specs, specs, row_recv).wait()
    for g in range(n_row):
        for n in range(H):
            for c in range(NC):
                coeff_ref[16 * g + 2 * n : 16 * g + 2 * n + 2, c * NS : (c + 1) * NS] = specs[
                    g, n * NC + c
                ]
    high, low = split(coeff_ref[...])
    for k in range(2):
        rhs_ref[2 * PAD * k : 2 * PAD * k + PAD, :] = high
        rhs_ref[2 * PAD * k + PAD : 2 * PAD * (k + 1), :] = low
    heard_ref[...] = dot(table_ref[...], rhs_ref[...])

    def gather(t, carry):
        heard = heard_ref[pl.ds(pl.multiple_of(t * NJ, NJ), NJ), :]
        heard = jnp.concatenate([heard[:, c * NS : (c + 1) * NS] for c in range(NC)], axis=0)
        x = upd_ref[at(t), :] + (step_size * coupling) * heard
        upd_ref[at(t), :] = x
        high, low = split(x)
        found = dot(jnp.concatenate([high, low], axis=1), cell_s[...])
        found = found.reshape(NC, NJ, NK) * cell_j[...]
        g_part[t] = jnp.sum(found, axis=1)
        return carry

    lax.fori_loop(0, NT, gather, 0)
    for t in range(NT):
        g_ref[t * NC : (t + 1) * NC, :] = g_part[t]

    for copy in halos:
        copy.wait_recv()
    inner = jnp.concatenate([pitch_in[0, 1], pitch_in[1, 0]], axis=1)
    high, low = split(inner)
    mixed = dot(mix_p[...], jnp.concatenate([high, low, high, low], axis=0))
    corr_ref[0] = -step_size * (
        -0.5 * mixed[:, 0:NS] + damping * (pitch_in[0, 0] - 4.0 * pitch_in[0, 1])
    )
    corr_ref[1] = (-step_size * damping) * pitch_in[0, 1]
    corr_ref[2] = (-step_size * damping) * pitch_in[1, 0]
    corr_ref[3] = -step_size * (
        0.5 * mixed[:, NS : 2 * NS] + damping * (pitch_in[1, 1] - 4.0 * pitch_in[1, 0])
    )

    high, low = split(corr_ref[0:4].reshape(4 * PAD, NS))
    found = dot(jnp.concatenate([high, low], axis=1), cell_s[...])
    total = g_ref[...]
    for e, at_row in enumerate((0, 1, NJ - 2, NJ - 1)):
        total = total + found[e * PAD : (e + 1) * PAD] * cell_j[at_row : at_row + 1, :]
    g_ref[...] = total

    @pl.when(below)
    def _():
        pl.semaphore_wait(answer, 1)
        right.start()

    @pl.when(s < n_span - 1)
    def _():
        left_in = pltpu.make_async_copy(span_in.at[1], span_in.at[1], span_recv.at[1])
        left_in.wait()

    @pl.when(s > 0)
    def _():
        right_in = pltpu.make_async_copy(span_in.at[0], span_in.at[0], span_recv.at[0])
        right_in.wait()

    from_left, from_right = span_in[0], span_in[1]
    x = jnp.concatenate(
        [
            jnp.where(e4 < 2, from_left, from_right),
            jnp.where(e4 < 2, pltpu.roll(from_left, NS - 2, 1), pltpu.roll(from_right, 2, 1)),
        ],
        axis=0,
    )
    y = jnp.where(e4 == 0, pltpu.roll(x, NS - 1, 1), jnp.where(e4 == 3, pltpu.roll(x, 1, 1), 0.0))
    sign = jnp.where(e4 == 0, -0.5, jnp.where(e4 == 3, 0.5, 0.0))
    high, low = split(y)
    mixed = dot(mix_s[...], jnp.concatenate([high, low, high, low], axis=0))
    corr_ref[4] = -step_size * (sign * mixed + damping * (x - 4.0 * y))

    high, low = split(corr_ref[4])
    total = g_ref[...] + dot(jnp.concatenate([high, low], axis=1), cell_edge[...])

    turn_ref[...] = jnp.concatenate([total, pltpu.roll(total, NK - 1, 1)], axis=0).T
    for i in range(half):
        outgoing[:, i, :] = turn_ref[pl.ds(2 * i, n_pitch, stride=handoff), :]

    line = min(8, n_pitch)

    def send(k, carry):
        q = (k % (n_pitch // line)) * line + k // (n_pitch // line)

        @pl.when(q != p)
        def _():
            pltpu.make_async_remote_copy(
                outgoing.at[q],
                arrived.at[p],
                wall_send,
                wall_recv,
                device_id=(r, q, s),
                device_id_type=MESH,
            ).start()

        return carry

    lax.fori_loop(0, n_pitch, send, 0)
    pltpu.make_async_copy(outgoing.at[p], arrived.at[p], wall_recv).start()

    for e, at_row in enumerate((0, 1, NJ - 2, NJ - 1)):
        rows = pl.ds(at_row, TC, stride=NJ)
        upd_ref[rows, :] = upd_ref[rows, :] + corr_ref[e, 0:TC, :]
    e_lane = iota((2 * NS, NS), 0) & 3
    to_column = one_hot(iota((2 * NS, NS), 1) == jnp.where(e_lane < 2, e_lane, NS - 4 + e_lane))
    own = lane // 4 == iota((NJ, NS), 0)
    for t in range(NT):
        spread = jnp.concatenate(
            [
                jnp.where(own, corr_ref[4, t * NC + c : t * NC + c + 1, :], 0.0)
                for c in range(NC)
            ],
            axis=0,
        )
        high, low = split(spread)
        rows = slice(t * NC * NJ, (t + 1) * NC * NJ)
        upd_ref[rows, :] = upd_ref[rows, :] + dot(
            jnp.concatenate([high, low], axis=1), to_column
        )

    pltpu.make_async_copy(arrived, arrived, wall_recv).wait()
    some = outgoing.at[pl.ds(0, n_pitch - 1)]
    pltpu.make_async_copy(some, some, wall_send).wait()
    for copy in halos + spectra:
        copy.wait_send()

    @pl.when(s < n_span - 1)
    def _():
        right.wait_send()

    @pl.when(s > 0)
    def _():
        left.wait_send()


def finish(sizes, upd_ref, arrived, slot_ref, out_hbm, wall_ref, sem):
    half = NK // sizes[1] // 2
    stores = []
    for i in range(PARTS):
        part = pl.ds(i * (ROWS // PARTS), ROWS // PARTS)
        copy = pltpu.make_async_copy(upd_ref.at[part], out_hbm.at[part], sem.at[i])
        copy.start()
        stores.append(copy)

    slots = jnp.concatenate([arrived[:, i, :] for i in range(half)], axis=0).T
    high, low = split(jnp.concatenate([slots[0:PAD], slots[PAD : 2 * PAD]], axis=1))
    placed = dot(jnp.concatenate([high, low], axis=0), slot_ref[...])
    placed = placed[0:PAD] + placed[PAD : 2 * PAD]
    for k in range(NK // NS):
        wall_ref[:, k, :] = placed[0:TC, k * NS : (k + 1) * NS]
    for copy in stores:
        copy.wait()


def local(sizes, unknowns, spectrum, blades, harmonics, pitch_jac, span_jac, send_cell, recv_order):
    n_row, n_pitch, n_span = sizes
    half = NK // n_pitch // 2
    vmem, dma = pltpu.VMEM, pltpu.SemaphoreType.DMA
    in_hbm = pl.BlockSpec(memory_space=pltpu.HBM)
    in_vmem = pl.BlockSpec(memory_space=pltpu.VMEM)
    smem = pltpu.SMEM
    updated, arrived, slots = pl.pallas_call(
        functools.partial(section, sizes),
        out_shape=(vmem((ROWS, NS), F32), vmem((n_pitch, half, NS), F32), vmem((NK, NK), BF16)),
        in_specs=[in_hbm] * 8,
        out_specs=(in_vmem, in_vmem, in_vmem),
        scratch_shapes=[
            smem((n_row,), I32),
            smem((n_row, H), I32),
            smem((NC, NC), F32),
            smem((NC, NC), F32),
            vmem((ROWS, NS), F32),
            vmem((NT * NJ, NC * NS), F32),
            vmem((n_row, H * NC, 2, NS), F32),
            vmem((PAD, NC * NS), F32),
            vmem((4 * PAD, NC * NS), BF16),
            vmem((NT * NJ, 2 * NS), BF16),
            vmem((1, NK), I32),
            vmem((1, NK), I32),
            vmem((2 * NS, NK), BF16),
            vmem((NJ, NK), F32),
            vmem((2 * NS, NK), BF16),
            vmem((PAD, 2 * NS), BF16),
            vmem((PAD, 2 * NS), BF16),
            vmem((2, 2, PAD, NS), F32),
            vmem((2, 2, PAD, NS), F32),
            vmem((2, PAD // 2, NS), F32),
            vmem((2, PAD // 2, NS), F32),
            vmem((PAD, NS), F32),
            vmem((5, PAD, NS), F32),
            vmem((NT, NC, NK), F32),
            vmem((PAD, NK), F32),
            vmem((NK, NS), F32),
            vmem((n_pitch, half, NS), F32),
            dma((PARTS + 6,)),
            dma((2,)),
            dma((2,)),
            dma((2,)),
            dma((2,)),
            dma((n_row,)),
            dma,
            dma,
            dma,
            pltpu.SemaphoreType.REGULAR,
        ],
        compiler_params=pltpu.CompilerParams(
            collective_id=1, has_side_effects=True, vmem_limit_bytes=32 * 1024 * 1024
        ),
        name="flux_section",
    )(
        *(
            pltpu.with_memory_space_constraint(x, pltpu.HBM)
            for x in (
                blades,
                harmonics,
                pitch_jac,
                span_jac,
                unknowns.reshape(ROWS, NS),
                jnp.transpose(spectrum[0], (1, 2, 0, 3)).reshape(H * NC, 2, NS),
                send_cell.reshape(1, NK),
                recv_order.reshape(1, NK),
            )
        )
    )
    updated, wall = pl.pallas_call(
        functools.partial(finish, sizes),
        out_shape=(
            jax.ShapeDtypeStruct((ROWS, NS), F32),
            jax.ShapeDtypeStruct((TC, NK // NS, NS), F32),
        ),
        in_specs=[in_vmem] * 3,
        out_specs=(in_hbm, in_vmem),
        scratch_shapes=[dma((PARTS,))],
        compiler_params=pltpu.CompilerParams(vmem_limit_bytes=8 * 1024 * 1024),
        name="wall_order",
    )(updated, arrived, slots)
    return (
        updated.reshape(unknowns.shape),
        wall.reshape(1, 1, NT, NC, NK),
    )


def solution(mesh):
    sizes = (mesh.shape["row"], mesh.shape["pitch"], mesh.shape["span"])
    return jax.shard_map(
        functools.partial(local, sizes),
        mesh=mesh,
        in_specs=(
            P("row", None, None, "pitch", "span"),
            P("row", None, None, None, "span"),
            P(),
            P(),
            P(),
            P(),
            P("row", "span", "pitch", None),
            P("row", "span", "pitch", None),
        ),
        out_specs=(P("row", None, None, "pitch", "span"), P("row", "span", None, None, "pitch")),
        check_vma=False,
    )
```

```python
import functools
import math

import jax
import jax.numpy as jnp
import numpy as np
from jax import lax
from jax.experimental import pallas as pl
from jax.experimental.pallas import tpu as pltpu
from jax.sharding import PartitionSpec as P

MESH = pl.DeviceIdType.MESH
F32, BF16, I32 = jnp.float32, jnp.bfloat16, jnp.int32

H = 5
NT = 11
NC = 5
NJ = 32
NS = 128
NK = 256
TC = NT * NC
PAD = 64
ROWS = TC * NJ
PARTS = 5

step_size = 0.25
damping = 1.0 / 16.0
coupling = 0.5
frequency = 0.5
far_weight = 0.5

d_entries = [
    float(np.float32(0.5 * frequency * math.cos(math.pi * n) / math.sin(math.pi * n / NT)))
    for n in range(1, NT // 2 + 1)
]


def iota(shape, dim):
    return lax.broadcasted_iota(I32, shape, dim)


def split(x):
    high = x.astype(BF16)
    return high, (x - high.astype(F32)).astype(BF16)


def dot(a, b):
    return lax.dot_general(a, b, (((1,), (0,)), ((), ())), preferred_element_type=F32)


def one_hot(condition):
    return jnp.where(condition, 1.0, 0.0).astype(BF16)


def section(
    sizes,
    blades_hbm,
    harmonics_hbm,
    pitch_jac_hbm,
    span_jac_hbm,
    u_hbm,
    spec_hbm,
    cell_hbm,
    order_hbm,
    upd_ref,
    arrived,
    slot_ref,
    blades,
    harmonics,
    pitch_jac,
    span_jac,
    u_ref,
    heard_ref,
    specs,
    coeff_ref,
    rhs_ref,
    table_ref,
    cell_ref,
    order_ref,
    cell_s,
    cell_j,
    cell_edge,
    mix_p,
    mix_s,
    pitch_out,
    pitch_in,
    span_out,
    span_in,
    edge_ref,
    corr_ref,
    g_part,
    g_ref,
    turn_ref,
    outgoing,
    load_sem,
    pitch_send,
    pitch_recv,
    span_send,
    span_recv,
    row_send,
    row_recv,
    wall_send,
    wall_recv,
    answer,
):
    n_row, n_pitch, n_span = sizes
    handoff = NK // n_pitch
    half = handoff // 2
    r, p, s = lax.axis_index("row"), lax.axis_index("pitch"), lax.axis_index("span")

    def pitch_peer(k):
        return (r, (p + k) & (n_pitch - 1), s)

    def row_peer(k):
        return (lax.rem(r + k, n_row), p, s)

    loads = []
    for i in range(PARTS):
        part = pl.ds(i * (ROWS // PARTS), ROWS // PARTS)
        copy = pltpu.make_async_copy(u_hbm.at[part], u_ref.at[part], load_sem.at[i])
        copy.start()
        loads.append(copy)

    middle = n_span // 2
    mate = s + 1 - 2 * lax.rem(s, 2)
    below, above = s == middle - 1, s == middle

    def span_peer(k):
        return (r, p, lax.rem(s + k + n_span, n_span))

    barrier = pltpu.get_barrier_semaphore()
    pl.semaphore_signal(barrier, inc=1, device_id=(r, p, mate), device_id_type=MESH)

    @pl.when(below)
    def _():
        pl.semaphore_signal(barrier, inc=1, device_id=span_peer(1), device_id_type=MESH)

    for k in (1, n_pitch - 1):
        pl.semaphore_signal(barrier, inc=1, device_id=pitch_peer(k), device_id_type=MESH)
    for k in range(1, n_row):
        pl.semaphore_signal(barrier, inc=1, device_id=row_peer(k), device_id_type=MESH)

    for k in range(2, n_pitch - 1):
        pl.semaphore_signal(barrier, inc=1, device_id=pitch_peer(k), device_id_type=MESH)

    lane = iota((1, NS), 1)

    for copy in loads:
        copy.wait()
    edges = jnp.zeros((TC, NS), F32)
    for j in range(NJ):
        turned = pltpu.roll(u_ref[pl.ds(j, TC, stride=NJ), :], (2 + 4 * j) % NS, 1)
        edges = jnp.where((lane >= 4 * j) & (lane < 4 * j + 4), turned, edges)
    edge_ref[0:TC, :] = edges
    edge_ref[TC:PAD, :] = jnp.zeros((PAD - TC, NS), F32)
    e4 = lax.rem(lane, 4)
    low, high = edge_ref[0 : PAD // 2, :], edge_ref[PAD // 2 : PAD, :]
    span_out[0] = jnp.where(e4 < 2, low, pltpu.roll(high, 2, 1))
    span_out[1] = jnp.where(e4 >= 2, low, pltpu.roll(high, NS - 2, 1))

    greeters = 1 + n_row - 1 + n_pitch - 1
    pl.semaphore_wait(barrier, jnp.where(above, greeters + 1, greeters))

    @pl.when(above)
    def _():
        pl.semaphore_signal(answer, inc=1, device_id=span_peer(-1), device_id_type=MESH)

    right = pltpu.make_async_remote_copy(
        span_out.at[0],
        span_in.at[0],
        span_send.at[0],
        span_recv.at[0],
        device_id=span_peer(1),
        device_id_type=MESH,
    )
    left = pltpu.make_async_remote_copy(
        span_out.at[1],
        span_in.at[1],
        span_send.at[1],
        span_recv.at[1],
        device_id=span_peer(-1),
        device_id_type=MESH,
    )

    @pl.when(s > 0)
    def _():
        left.start()

    @pl.when((s < n_span - 1) & (s != middle - 1))
    def _():
        right.start()

    scalars = []
    for i, (src, dst) in enumerate(
        (
            (blades_hbm, blades),
            (harmonics_hbm, harmonics),
            (pitch_jac_hbm, pitch_jac),
            (span_jac_hbm, span_jac),
            (cell_hbm, cell_ref),
            (order_hbm, order_ref),
        )
    ):
        copy = pltpu.make_async_copy(src, dst, load_sem.at[PARTS + i])
        copy.start()
        scalars.append(copy)

    pitch_out[:, :, TC:PAD, :] = jnp.zeros((2, 2, PAD - TC, NS), F32)
    for layer in range(2):
        pitch_out[0, layer, 0:TC, :] = u_ref[pl.ds(NJ - 2 + layer, TC, stride=NJ), :]
        pitch_out[1, layer, 0:TC, :] = u_ref[pl.ds(layer, TC, stride=NJ), :]

    halos = []
    for way, k in ((0, 1), (1, n_pitch - 1)):
        copy = pltpu.make_async_remote_copy(
            pitch_out.at[way],
            pitch_in.at[way],
            pitch_send.at[way],
            pitch_recv.at[way],
            device_id=pitch_peer(k),
            device_id_type=MESH,
        )
        copy.start()
        halos.append(copy)
    spectra = []
    for k in range(1, n_row):
        copy = pltpu.make_async_remote_copy(
            spec_hbm,
            specs.at[r],
            row_send.at[k],
            row_recv,
            device_id=row_peer(k),
            device_id_type=MESH,
        )
        copy.start()
        spectra.append(copy)
    pltpu.make_async_copy(spec_hbm, specs.at[r], row_recv).start()

    g_ref[TC:PAD, :] = jnp.zeros((PAD - TC, NK), F32)
    coeff_ref[...] = jnp.zeros_like(coeff_ref)

    @pl.when(s == 0)
    def _():
        span_in[0] = jnp.zeros_like(span_in[0])

    @pl.when(s == n_span - 1)
    def _():
        span_in[1] = jnp.zeros_like(span_in[1])

    for copy in scalars:
        copy.wait()
    cell = cell_ref[...]
    cj, cs = cell // NS, lax.rem(cell, NS)
    cell_s[...] = one_hot((iota((2 * NS, NK), 0) & (NS - 1)) == cs)
    cell_j[...] = jnp.where(iota((NJ, NK), 0) == cj, 1.0, 0.0)
    place = iota((2 * NS, NK), 0) & (NS - 1)
    e_row = place & 3
    column = jnp.where(e_row < 2, e_row, NS - 4 + e_row)
    cell_edge[...] = one_hot((place // 4 == cj) & (column == cs))
    rho = iota((NK, NK), 0)
    rest = rho & (NS - 1)
    slot = (rest & (n_pitch - 1)) * handoff + (rest // n_pitch) * 2 + rho // NS
    slot_ref[...] = one_hot(slot == order_ref[...])

    mr, mc = iota((PAD, NS), 0), iota((PAD, NS), 1) & (PAD - 1)
    tr, tcol = (mr * 205) >> 10, (mc * 205) >> 10
    cr, cc = mr - 5 * tr, mc - 5 * tcol
    same = (tr == tcol) & (mr < TC) & (mc < TC)
    pair = jnp.where(same, cr * NC + cc, -1)
    for jac, mix in ((pitch_jac, mix_p), (span_jac, mix_s)):
        m = jnp.zeros((PAD, NS), F32)
        for a in range(NC):
            for c in range(NC):
                m = jnp.where(pair == a * NC + c, jac[a, c], m)
        mh, ml = split(m)
        mix[:, 0:NS] = mh
        mix[:, NS : 2 * NS] = ml

    l64 = lane & (PAD - 1)
    lg, lk = l64 // 16, l64 & 15
    order_of = jnp.zeros((1, NS), I32)
    turns_of = jnp.zeros((1, NS), I32)
    weight = jnp.zeros((1, NS), F32)
    for g in range(n_row):
        distance = jnp.abs(r - g)
        w = jnp.where(distance == 1, 1.0, jnp.where(distance >= 2, far_weight, 0.0)).astype(F32)
        weight = jnp.where((lg == g) & (lk < 2 * H), w, weight)
        for n in range(H):
            here = (lg == g) & (lk // 2 == n)
            order_of = jnp.where(here, harmonics[g, n], order_of)
            turns_of = jnp.where(here, harmonics[g, n] * blades[g], turns_of)
    whole = n_pitch * NJ
    cells = p * NJ + iota((NJ, NS), 0)
    phase_j = ((turns_of * cells) & (whole - 1)).astype(F32) * (2.0 * math.pi / whole)
    phase_j = phase_j - (lk & 1).astype(F32) * (0.5 * math.pi)
    times = order_of * iota((16, NS), 0)
    times = times - NT * ((times * 5958) >> 16)
    phase_t = times.astype(F32) * (2.0 * math.pi / NT)
    cos_j, sin_j = weight * jnp.cos(phase_j), weight * jnp.sin(phase_j)
    cos_t, sin_t = jnp.cos(phase_t), jnp.sin(phase_t)
    for t in range(NT):
        high, low = split(cos_t[t : t + 1] * cos_j - sin_t[t : t + 1] * sin_j)
        table_ref[t * NJ : (t + 1) * NJ, 0:NS] = high
        table_ref[t * NJ : (t + 1) * NJ, NS : 2 * NS] = low

    row = iota((1, NJ, 1), 1)

    def at(t):
        return pl.ds(pl.multiple_of(t * (NC * NJ), NC * NJ), NC * NJ)

    def interior(t, carry):
        x = u_ref[at(t), :]
        m1 = jnp.where(lane >= 1, pltpu.roll(x, 1, 1), 0.0)
        m2 = jnp.where(lane >= 2, pltpu.roll(x, 2, 1), 0.0)
        p1 = jnp.where(lane < NS - 1, pltpu.roll(x, NS - 1, 1), 0.0)
        p2 = jnp.where(lane < NS - 2, pltpu.roll(x, NS - 2, 1), 0.0)
        d1s = (0.5 * (p1 - m1)).reshape(NC, NJ, NS)
        fourth = ((p2 + m2) - 4.0 * (p1 + m1)).reshape(NC, NJ, NS)
        x = x.reshape(NC, NJ, NS)
        m1 = jnp.where(row >= 1, pltpu.roll(x, 1, 1), 0.0)
        m2 = jnp.where(row >= 2, pltpu.roll(x, 2, 1), 0.0)
        p1 = jnp.where(row < NJ - 1, pltpu.roll(x, NJ - 1, 1), 0.0)
        p2 = jnp.where(row < NJ - 2, pltpu.roll(x, NJ - 2, 1), 0.0)
        d1p = 0.5 * (p1 - m1)
        fourth = fourth + ((p2 + m2) - 4.0 * (p1 + m1))
        change = damping * fourth + (12.0 * damping + 2.0 * coupling) * x
        for n in range(1, NT // 2 + 1):
            before = u_ref[at(lax.rem(t + NT - n, NT)), :]
            after = u_ref[at(lax.rem(t + n, NT)), :]
            change = change + d_entries[n - 1] * (before - after).reshape(NC, NJ, NS)
        for a in range(NC):
            flux = change[a]
            for c in range(NC):
                flux = flux + pitch_jac[a, c] * d1p[c] + span_jac[a, c] * d1s[c]
            upd_ref[pl.ds(pl.multiple_of((t * NC + a) * NJ, NJ), NJ), :] = x[a] - step_size * flux
        return carry

    lax.fori_loop(0, NT, interior, 0)

    pltpu.make_async_copy(specs, specs, row_recv).wait()
    for g in range(n_row):
        for n in range(H):
            for c in range(NC):
                coeff_ref[16 * g + 2 * n : 16 * g + 2 * n + 2, c * NS : (c + 1) * NS] = specs[
                    g, n * NC + c
                ]
    high, low = split(coeff_ref[...])
    for k in range(2):
        rhs_ref[2 * PAD * k : 2 * PAD * k + PAD, :] = high
        rhs_ref[2 * PAD * k + PAD : 2 * PAD * (k + 1), :] = low
    heard_ref[...] = dot(table_ref[...], rhs_ref[...])

    def gather(t, carry):
        heard = heard_ref[pl.ds(pl.multiple_of(t * NJ, NJ), NJ), :]
        heard = jnp.concatenate([heard[:, c * NS : (c + 1) * NS] for c in range(NC)], axis=0)
        x = upd_ref[at(t), :] + (step_size * coupling) * heard
        upd_ref[at(t), :] = x
        high, low = split(x)
        found = dot(jnp.concatenate([high, low], axis=1), cell_s[...])
        found = found.reshape(NC, NJ, NK) * cell_j[...]
        g_part[t] = jnp.sum(found, axis=1)
        return carry

    lax.fori_loop(0, NT, gather, 0)
    for t in range(NT):
        g_ref[t * NC : (t + 1) * NC, :] = g_part[t]

    for copy in halos:
        copy.wait_recv()
    inner = jnp.concatenate([pitch_in[0, 1], pitch_in[1, 0]], axis=1)
    high, low = split(inner)
    mixed = dot(mix_p[...], jnp.concatenate([high, low, high, low], axis=0))
    corr_ref[0] = -step_size * (
        -0.5 * mixed[:, 0:NS] + damping * (pitch_in[0, 0] - 4.0 * pitch_in[0, 1])
    )
    corr_ref[1] = (-step_size * damping) * pitch_in[0, 1]
    corr_ref[2] = (-step_size * damping) * pitch_in[1, 0]
    corr_ref[3] = -step_size * (
        0.5 * mixed[:, NS : 2 * NS] + damping * (pitch_in[1, 1] - 4.0 * pitch_in[1, 0])
    )

    high, low = split(corr_ref[0:4].reshape(4 * PAD, NS))
    found = dot(jnp.concatenate([high, low], axis=1), cell_s[...])
    total = g_ref[...]
    for e, at_row in enumerate((0, 1, NJ - 2, NJ - 1)):
        total = total + found[e * PAD : (e + 1) * PAD] * cell_j[at_row : at_row + 1, :]
    g_ref[...] = total

    @pl.when(below)
    def _():
        pl.semaphore_wait(answer, 1)
        right.start()

    @pl.when(s < n_span - 1)
    def _():
        left_in = pltpu.make_async_copy(span_in.at[1], span_in.at[1], span_recv.at[1])
        left_in.wait()

    @pl.when(s > 0)
    def _():
        right_in = pltpu.make_async_copy(span_in.at[0], span_in.at[0], span_recv.at[0])
        right_in.wait()

    from_left, from_right = span_in[0], span_in[1]
    x = jnp.concatenate(
        [
            jnp.where(e4 < 2, from_left, from_right),
            jnp.where(e4 < 2, pltpu.roll(from_left, NS - 2, 1), pltpu.roll(from_right, 2, 1)),
        ],
        axis=0,
    )
    y = jnp.where(e4 == 0, pltpu.roll(x, NS - 1, 1), jnp.where(e4 == 3, pltpu.roll(x, 1, 1), 0.0))
    sign = jnp.where(e4 == 0, -0.5, jnp.where(e4 == 3, 0.5, 0.0))
    high, low = split(y)
    mixed = dot(mix_s[...], jnp.concatenate([high, low, high, low], axis=0))
    corr_ref[4] = -step_size * (sign * mixed + damping * (x - 4.0 * y))

    high, low = split(corr_ref[4])
    total = g_ref[...] + dot(jnp.concatenate([high, low], axis=1), cell_edge[...])

    turn_ref[...] = jnp.concatenate([total, pltpu.roll(total, NK - 1, 1)], axis=0).T
    for i in range(half):
        outgoing[:, i, :] = turn_ref[pl.ds(2 * i, n_pitch, stride=handoff), :]

    line = min(8, n_pitch)

    def send(z, carry):
        for y in range(n_pitch // line):
            q = y * line + z

            @pl.when(q != p)
            def _():
                pltpu.make_async_remote_copy(
                    outgoing.at[q],
                    arrived.at[p],
                    wall_send,
                    wall_recv,
                    device_id=(r, q, s),
                    device_id_type=MESH,
                ).start()

        return carry

    lax.fori_loop(0, line, send, 0)
    pltpu.make_async_copy(outgoing.at[p], arrived.at[p], wall_recv).start()

    for e, at_row in enumerate((0, 1, NJ - 2, NJ - 1)):
        rows = pl.ds(at_row, TC, stride=NJ)
        upd_ref[rows, :] = upd_ref[rows, :] + corr_ref[e, 0:TC, :]
    e_lane = iota((2 * NS, NS), 0) & 3
    to_column = one_hot(iota((2 * NS, NS), 1) == jnp.where(e_lane < 2, e_lane, NS - 4 + e_lane))
    own = lane // 4 == iota((NJ, NS), 0)
    for t in range(NT):
        spread = jnp.concatenate(
            [
                jnp.where(own, corr_ref[4, t * NC + c : t * NC + c + 1, :], 0.0)
                for c in range(NC)
            ],
            axis=0,
        )
        high, low = split(spread)
        rows = slice(t * NC * NJ, (t + 1) * NC * NJ)
        upd_ref[rows, :] = upd_ref[rows, :] + dot(
            jnp.concatenate([high, low], axis=1), to_column
        )

    pltpu.make_async_copy(arrived, arrived, wall_recv).wait()
    some = outgoing.at[pl.ds(0, n_pitch - 1)]
    pltpu.make_async_copy(some, some, wall_send).wait()
    for copy in halos + spectra:
        copy.wait_send()

    @pl.when(s < n_span - 1)
    def _():
        right.wait_send()

    @pl.when(s > 0)
    def _():
        left.wait_send()


def finish(sizes, upd_ref, arrived, slot_ref, out_hbm, wall_ref, sem):
    half = NK // sizes[1] // 2
    stores = []
    for i in range(PARTS):
        part = pl.ds(i * (ROWS // PARTS), ROWS // PARTS)
        copy = pltpu.make_async_copy(upd_ref.at[part], out_hbm.at[part], sem.at[i])
        copy.start()
        stores.append(copy)

    slots = jnp.concatenate([arrived[:, i, :] for i in range(half)], axis=0).T
    high, low = split(jnp.concatenate([slots[0:PAD], slots[PAD : 2 * PAD]], axis=1))
    placed = dot(jnp.concatenate([high, low], axis=0), slot_ref[...])
    placed = placed[0:PAD] + placed[PAD : 2 * PAD]
    for k in range(NK // NS):
        wall_ref[:, k, :] = placed[0:TC, k * NS : (k + 1) * NS]
    for copy in stores:
        copy.wait()


def local(sizes, unknowns, spectrum, blades, harmonics, pitch_jac, span_jac, send_cell, recv_order):
    n_row, n_pitch, n_span = sizes
    half = NK // n_pitch // 2
    vmem, dma = pltpu.VMEM, pltpu.SemaphoreType.DMA
    in_hbm = pl.BlockSpec(memory_space=pltpu.HBM)
    in_vmem = pl.BlockSpec(memory_space=pltpu.VMEM)
    smem = pltpu.SMEM
    updated, arrived, slots = pl.pallas_call(
        functools.partial(section, sizes),
        out_shape=(vmem((ROWS, NS), F32), vmem((n_pitch, half, NS), F32), vmem((NK, NK), BF16)),
        in_specs=[in_hbm] * 8,
        out_specs=(in_vmem, in_vmem, in_vmem),
        scratch_shapes=[
            smem((n_row,), I32),
            smem((n_row, H), I32),
            smem((NC, NC), F32),
            smem((NC, NC), F32),
            vmem((ROWS, NS), F32),
            vmem((NT * NJ, NC * NS), F32),
            vmem((n_row, H * NC, 2, NS), F32),
            vmem((PAD, NC * NS), F32),
            vmem((4 * PAD, NC * NS), BF16),
            vmem((NT * NJ, 2 * NS), BF16),
            vmem((1, NK), I32),
            vmem((1, NK), I32),
            vmem((2 * NS, NK), BF16),
            vmem((NJ, NK), F32),
            vmem((2 * NS, NK), BF16),
            vmem((PAD, 2 * NS), BF16),
            vmem((PAD, 2 * NS), BF16),
            vmem((2, 2, PAD, NS), F32),
            vmem((2, 2, PAD, NS), F32),
            vmem((2, PAD // 2, NS), F32),
            vmem((2, PAD // 2, NS), F32),
            vmem((PAD, NS), F32),
            vmem((5, PAD, NS), F32),
            vmem((NT, NC, NK), F32),
            vmem((PAD, NK), F32),
            vmem((NK, NS), F32),
            vmem((n_pitch, half, NS), F32),
            dma((PARTS + 6,)),
            dma((2,)),
            dma((2,)),
            dma((2,)),
            dma((2,)),
            dma((n_row,)),
            dma,
            dma,
            dma,
            pltpu.SemaphoreType.REGULAR,
        ],
        compiler_params=pltpu.CompilerParams(
            collective_id=1, has_side_effects=True, vmem_limit_bytes=32 * 1024 * 1024
        ),
        name="flux_section",
    )(
        *(
            pltpu.with_memory_space_constraint(x, pltpu.HBM)
            for x in (
                blades,
                harmonics,
                pitch_jac,
                span_jac,
                unknowns.reshape(ROWS, NS),
                jnp.transpose(spectrum[0], (1, 2, 0, 3)).reshape(H * NC, 2, NS),
                send_cell.reshape(1, NK),
                recv_order.reshape(1, NK),
            )
        )
    )
    updated, wall = pl.pallas_call(
        functools.partial(finish, sizes),
        out_shape=(
            jax.ShapeDtypeStruct((ROWS, NS), F32),
            jax.ShapeDtypeStruct((TC, NK // NS, NS), F32),
        ),
        in_specs=[in_vmem] * 3,
        out_specs=(in_hbm, in_vmem),
        scratch_shapes=[dma((PARTS,))],
        compiler_params=pltpu.CompilerParams(vmem_limit_bytes=8 * 1024 * 1024),
        name="wall_order",
    )(updated, arrived, slots)
    return (
        updated.reshape(unknowns.shape),
        wall.reshape(1, 1, NT, NC, NK),
    )


def solution(mesh):
    sizes = (mesh.shape["row"], mesh.shape["pitch"], mesh.shape["span"])
    return jax.shard_map(
        functools.partial(local, sizes),
        mesh=mesh,
        in_specs=(
            P("row", None, None, "pitch", "span"),
            P("row", None, None, None, "span"),
            P(),
            P(),
            P(),
            P(),
            P("row", "span", "pitch", None),
            P("row", "span", "pitch", None),
        ),
        out_specs=(P("row", None, None, "pitch", "span"), P("row", "span", None, None, "pitch")),
        check_vma=False,
    )
```

```python
import functools
import math

import jax
import jax.numpy as jnp
import numpy as np
from jax import lax
from jax.experimental import pallas as pl
from jax.experimental.pallas import tpu as pltpu
from jax.sharding import PartitionSpec as P

MESH = pl.DeviceIdType.MESH
F32, BF16, I32 = jnp.float32, jnp.bfloat16, jnp.int32

H = 5
NT = 11
NC = 5
NJ = 32
NS = 128
NK = 256
TC = NT * NC
PAD = 64
ROWS = TC * NJ
PARTS = 5

step_size = 0.25
damping = 1.0 / 16.0
coupling = 0.5
frequency = 0.5
far_weight = 0.5

d_entries = [
    float(np.float32(0.5 * frequency * math.cos(math.pi * n) / math.sin(math.pi * n / NT)))
    for n in range(1, NT // 2 + 1)
]


def iota(shape, dim):
    return lax.broadcasted_iota(I32, shape, dim)


def split(x):
    high = x.astype(BF16)
    return high, (x - high.astype(F32)).astype(BF16)


def dot(a, b):
    return lax.dot_general(a, b, (((1,), (0,)), ((), ())), preferred_element_type=F32)


def one_hot(condition):
    return jnp.where(condition, 1.0, 0.0).astype(BF16)


def section(
    sizes,
    blades_hbm,
    harmonics_hbm,
    pitch_jac_hbm,
    span_jac_hbm,
    u_hbm,
    spec_hbm,
    cell_hbm,
    order_hbm,
    upd_ref,
    arrived,
    slot_ref,
    blades,
    harmonics,
    pitch_jac,
    span_jac,
    u_ref,
    heard_ref,
    specs,
    coeff_ref,
    rhs_ref,
    table_ref,
    cell_ref,
    order_ref,
    cell_s,
    cell_j,
    cell_edge,
    mix_p,
    mix_s,
    pitch_out,
    pitch_in,
    span_out,
    span_in,
    edge_ref,
    corr_ref,
    g_part,
    g_ref,
    turn_ref,
    outgoing,
    load_sem,
    pitch_send,
    pitch_recv,
    span_send,
    span_recv,
    row_send,
    row_recv,
    wall_send,
    wall_recv,
    answer,
):
    n_row, n_pitch, n_span = sizes
    handoff = NK // n_pitch
    half = handoff // 2
    r, p, s = lax.axis_index("row"), lax.axis_index("pitch"), lax.axis_index("span")

    def pitch_peer(k):
        return (r, lax.rem(p + k, n_pitch), s)

    def row_peer(k):
        return (lax.rem(r + k, n_row), p, s)

    loads = []
    for i in range(PARTS):
        part = pl.ds(i * (ROWS // PARTS), ROWS // PARTS)
        copy = pltpu.make_async_copy(u_hbm.at[part], u_ref.at[part], load_sem.at[i])
        copy.start()
        loads.append(copy)

    middle = n_span // 2
    mate = s + 1 - 2 * lax.rem(s, 2)
    below, above = s == middle - 1, s == middle

    def span_peer(k):
        return (r, p, lax.rem(s + k + n_span, n_span))

    barrier = pltpu.get_barrier_semaphore()
    pl.semaphore_signal(barrier, inc=1, device_id=(r, p, mate), device_id_type=MESH)

    @pl.when(below)
    def _():
        pl.semaphore_signal(barrier, inc=1, device_id=span_peer(1), device_id_type=MESH)

    for k in (1, n_pitch - 1):
        pl.semaphore_signal(barrier, inc=1, device_id=pitch_peer(k), device_id_type=MESH)
    for k in range(1, n_row):
        pl.semaphore_signal(barrier, inc=1, device_id=row_peer(k), device_id_type=MESH)

    def greet(k, carry):
        pl.semaphore_signal(barrier, inc=1, device_id=pitch_peer(k), device_id_type=MESH)
        return carry

    lax.fori_loop(2, n_pitch - 1, greet, 0)

    scalars = []
    for i, (src, dst) in enumerate(
        (
            (blades_hbm, blades),
            (harmonics_hbm, harmonics),
            (pitch_jac_hbm, pitch_jac),
            (span_jac_hbm, span_jac),
            (cell_hbm, cell_ref),
            (order_hbm, order_ref),
        )
    ):
        copy = pltpu.make_async_copy(src, dst, load_sem.at[PARTS + i])
        copy.start()
        scalars.append(copy)

    lane = iota((1, NS), 1)

    for copy in loads:
        copy.wait()
    edges = jnp.zeros((TC, NS), F32)
    for j in range(NJ):
        turned = pltpu.roll(u_ref[pl.ds(j, TC, stride=NJ), :], (2 + 4 * j) % NS, 1)
        edges = jnp.where((lane >= 4 * j) & (lane < 4 * j + 4), turned, edges)
    edge_ref[0:TC, :] = edges
    edge_ref[TC:PAD, :] = jnp.zeros((PAD - TC, NS), F32)
    e4 = lax.rem(lane, 4)
    low, high = edge_ref[0 : PAD // 2, :], edge_ref[PAD // 2 : PAD, :]
    span_out[0] = jnp.where(e4 < 2, low, pltpu.roll(high, 2, 1))
    span_out[1] = jnp.where(e4 >= 2, low, pltpu.roll(high, NS - 2, 1))

    greeters = 1 + n_row - 1 + n_pitch - 1
    pl.semaphore_wait(barrier, jnp.where(above, greeters + 1, greeters))

    @pl.when(above)
    def _():
        pl.semaphore_signal(answer, inc=1, device_id=span_peer(-1), device_id_type=MESH)

    right = pltpu.make_async_remote_copy(
        span_out.at[0],
        span_in.at[0],
        span_send.at[0],
        span_recv.at[0],
        device_id=span_peer(1),
        device_id_type=MESH,
    )
    left = pltpu.make_async_remote_copy(
        span_out.at[1],
        span_in.at[1],
        span_send.at[1],
        span_recv.at[1],
        device_id=span_peer(-1),
        device_id_type=MESH,
    )

    @pl.when(s > 0)
    def _():
        left.start()

    @pl.when((s < n_span - 1) & (s != middle - 1))
    def _():
        right.start()

    pitch_out[:, :, TC:PAD, :] = jnp.zeros((2, 2, PAD - TC, NS), F32)
    for layer in range(2):
        pitch_out[0, layer, 0:TC, :] = u_ref[pl.ds(NJ - 2 + layer, TC, stride=NJ), :]
        pitch_out[1, layer, 0:TC, :] = u_ref[pl.ds(layer, TC, stride=NJ), :]

    halos = []
    for way, k in ((0, 1), (1, n_pitch - 1)):
        copy = pltpu.make_async_remote_copy(
            pitch_out.at[way],
            pitch_in.at[way],
            pitch_send.at[way],
            pitch_recv.at[way],
            device_id=pitch_peer(k),
            device_id_type=MESH,
        )
        halos.append(copy)

    @pl.when(s < middle)
    def _():
        for copy in halos:
            copy.start()

    spectra = []
    for k in range(1, n_row):
        copy = pltpu.make_async_remote_copy(
            spec_hbm,
            specs.at[r],
            row_send.at[k],
            row_recv,
            device_id=row_peer(k),
            device_id_type=MESH,
        )
        copy.start()
        spectra.append(copy)
    pltpu.make_async_copy(spec_hbm, specs.at[r], row_recv).start()

    g_ref[TC:PAD, :] = jnp.zeros((PAD - TC, NK), F32)
    coeff_ref[...] = jnp.zeros_like(coeff_ref)

    @pl.when(s == 0)
    def _():
        span_in[0] = jnp.zeros_like(span_in[0])

    @pl.when(s == n_span - 1)
    def _():
        span_in[1] = jnp.zeros_like(span_in[1])

    for copy in scalars:
        copy.wait()
    cell = cell_ref[...]
    cj, cs = cell // NS, lax.rem(cell, NS)
    cell_s[...] = one_hot((iota((2 * NS, NK), 0) & (NS - 1)) == cs)
    cell_j[...] = jnp.where(iota((NJ, NK), 0) == cj, 1.0, 0.0)
    place = iota((2 * NS, NK), 0) & (NS - 1)
    e_row = place & 3
    column = jnp.where(e_row < 2, e_row, NS - 4 + e_row)
    cell_edge[...] = one_hot((place // 4 == cj) & (column == cs))
    rho = iota((NK, NK), 0)
    rest = rho & (NS - 1)
    slot = (rest & (n_pitch - 1)) * handoff + (rest // n_pitch) * 2 + rho // NS
    slot_ref[...] = one_hot(slot == order_ref[...])

    mr, mc = iota((PAD, NS), 0), iota((PAD, NS), 1) & (PAD - 1)
    tr, tcol = (mr * 205) >> 10, (mc * 205) >> 10
    cr, cc = mr - 5 * tr, mc - 5 * tcol
    same = (tr == tcol) & (mr < TC) & (mc < TC)
    pair = jnp.where(same, cr * NC + cc, -1)
    for jac, mix in ((pitch_jac, mix_p), (span_jac, mix_s)):
        m = jnp.zeros((PAD, NS), F32)
        for a in range(NC):
            for c in range(NC):
                m = jnp.where(pair == a * NC + c, jac[a, c], m)
        mh, ml = split(m)
        mix[:, 0:NS] = mh
        mix[:, NS : 2 * NS] = ml

    l64 = lane & (PAD - 1)
    lg, lk = l64 // 16, l64 & 15
    order_of = jnp.zeros((1, NS), I32)
    turns_of = jnp.zeros((1, NS), I32)
    weight = jnp.zeros((1, NS), F32)
    for g in range(n_row):
        distance = jnp.abs(r - g)
        w = jnp.where(distance == 1, 1.0, jnp.where(distance >= 2, far_weight, 0.0)).astype(F32)
        weight = jnp.where((lg == g) & (lk < 2 * H), w, weight)
        for n in range(H):
            here = (lg == g) & (lk // 2 == n)
            order_of = jnp.where(here, harmonics[g, n], order_of)
            turns_of = jnp.where(here, harmonics[g, n] * blades[g], turns_of)
    whole = n_pitch * NJ
    cells = p * NJ + iota((NJ, NS), 0)
    phase_j = ((turns_of * cells) & (whole - 1)).astype(F32) * (2.0 * math.pi / whole)
    phase_j = phase_j - (lk & 1).astype(F32) * (0.5 * math.pi)
    times = order_of * iota((16, NS), 0)
    times = times - NT * ((times * 5958) >> 16)
    phase_t = times.astype(F32) * (2.0 * math.pi / NT)
    cos_j, sin_j = weight * jnp.cos(phase_j), weight * jnp.sin(phase_j)
    cos_t, sin_t = jnp.cos(phase_t), jnp.sin(phase_t)
    for t in range(NT):
        high, low = split(cos_t[t : t + 1] * cos_j - sin_t[t : t + 1] * sin_j)
        table_ref[t * NJ : (t + 1) * NJ, 0:NS] = high
        table_ref[t * NJ : (t + 1) * NJ, NS : 2 * NS] = low

    row = iota((1, NJ, 1), 1)

    def at(t):
        return pl.ds(pl.multiple_of(t * (NC * NJ), NC * NJ), NC * NJ)

    def interior(t, carry):
        x = u_ref[at(t), :]
        m1 = jnp.where(lane >= 1, pltpu.roll(x, 1, 1), 0.0)
        m2 = jnp.where(lane >= 2, pltpu.roll(x, 2, 1), 0.0)
        p1 = jnp.where(lane < NS - 1, pltpu.roll(x, NS - 1, 1), 0.0)
        p2 = jnp.where(lane < NS - 2, pltpu.roll(x, NS - 2, 1), 0.0)
        d1s = (0.5 * (p1 - m1)).reshape(NC, NJ, NS)
        fourth = ((p2 + m2) - 4.0 * (p1 + m1)).reshape(NC, NJ, NS)
        x = x.reshape(NC, NJ, NS)
        m1 = jnp.where(row >= 1, pltpu.roll(x, 1, 1), 0.0)
        m2 = jnp.where(row >= 2, pltpu.roll(x, 2, 1), 0.0)
        p1 = jnp.where(row < NJ - 1, pltpu.roll(x, NJ - 1, 1), 0.0)
        p2 = jnp.where(row < NJ - 2, pltpu.roll(x, NJ - 2, 1), 0.0)
        d1p = 0.5 * (p1 - m1)
        fourth = fourth + ((p2 + m2) - 4.0 * (p1 + m1))
        change = damping * fourth + (12.0 * damping + 2.0 * coupling) * x
        for n in range(1, NT // 2 + 1):
            before = u_ref[at(lax.rem(t + NT - n, NT)), :]
            after = u_ref[at(lax.rem(t + n, NT)), :]
            change = change + d_entries[n - 1] * (before - after).reshape(NC, NJ, NS)
        for a in range(NC):
            flux = change[a]
            for c in range(NC):
                flux = flux + pitch_jac[a, c] * d1p[c] + span_jac[a, c] * d1s[c]
            upd_ref[pl.ds(pl.multiple_of((t * NC + a) * NJ, NJ), NJ), :] = x[a] - step_size * flux
        return carry

    lax.fori_loop(0, NT, interior, 0)

    @pl.when(s >= middle)
    def _():
        for copy in halos:
            copy.start()


    pltpu.make_async_copy(specs, specs, row_recv).wait()
    for g in range(n_row):
        for n in range(H):
            for c in range(NC):
                coeff_ref[16 * g + 2 * n : 16 * g + 2 * n + 2, c * NS : (c + 1) * NS] = specs[
                    g, n * NC + c
                ]
    high, low = split(coeff_ref[...])
    for k in range(2):
        rhs_ref[2 * PAD * k : 2 * PAD * k + PAD, :] = high
        rhs_ref[2 * PAD * k + PAD : 2 * PAD * (k + 1), :] = low
    heard_ref[...] = dot(table_ref[...], rhs_ref[...])

    def gather(t, carry):
        heard = heard_ref[pl.ds(pl.multiple_of(t * NJ, NJ), NJ), :]
        heard = jnp.concatenate([heard[:, c * NS : (c + 1) * NS] for c in range(NC)], axis=0)
        x = upd_ref[at(t), :] + (step_size * coupling) * heard
        upd_ref[at(t), :] = x
        high, low = split(x)
        found = dot(jnp.concatenate([high, low], axis=1), cell_s[...])
        found = found.reshape(NC, NJ, NK) * cell_j[...]
        g_part[t] = jnp.sum(found, axis=1)
        return carry

    lax.fori_loop(0, NT, gather, 0)
    for t in range(NT):
        g_ref[t * NC : (t + 1) * NC, :] = g_part[t]

    for copy in halos:
        copy.wait_recv()
    inner = jnp.concatenate([pitch_in[0, 1], pitch_in[1, 0]], axis=1)
    high, low = split(inner)
    mixed = dot(mix_p[...], jnp.concatenate([high, low, high, low], axis=0))
    corr_ref[0] = -step_size * (
        -0.5 * mixed[:, 0:NS] + damping * (pitch_in[0, 0] - 4.0 * pitch_in[0, 1])
    )
    corr_ref[1] = (-step_size * damping) * pitch_in[0, 1]
    corr_ref[2] = (-step_size * damping) * pitch_in[1, 0]
    corr_ref[3] = -step_size * (
        0.5 * mixed[:, NS : 2 * NS] + damping * (pitch_in[1, 1] - 4.0 * pitch_in[1, 0])
    )

    high, low = split(corr_ref[0:4].reshape(4 * PAD, NS))
    found = dot(jnp.concatenate([high, low], axis=1), cell_s[...])
    total = g_ref[...]
    for e, at_row in enumerate((0, 1, NJ - 2, NJ - 1)):
        total = total + found[e * PAD : (e + 1) * PAD] * cell_j[at_row : at_row + 1, :]
    g_ref[...] = total

    @pl.when(below)
    def _():
        pl.semaphore_wait(answer, 1)
        right.start()

    @pl.when(s < n_span - 1)
    def _():
        left_in = pltpu.make_async_copy(span_in.at[1], span_in.at[1], span_recv.at[1])
        left_in.wait()

    @pl.when(s > 0)
    def _():
        right_in = pltpu.make_async_copy(span_in.at[0], span_in.at[0], span_recv.at[0])
        right_in.wait()

    from_left, from_right = span_in[0], span_in[1]
    x = jnp.concatenate(
        [
            jnp.where(e4 < 2, from_left, from_right),
            jnp.where(e4 < 2, pltpu.roll(from_left, NS - 2, 1), pltpu.roll(from_right, 2, 1)),
        ],
        axis=0,
    )
    y = jnp.where(e4 == 0, pltpu.roll(x, NS - 1, 1), jnp.where(e4 == 3, pltpu.roll(x, 1, 1), 0.0))
    sign = jnp.where(e4 == 0, -0.5, jnp.where(e4 == 3, 0.5, 0.0))
    high, low = split(y)
    mixed = dot(mix_s[...], jnp.concatenate([high, low, high, low], axis=0))
    corr_ref[4] = -step_size * (sign * mixed + damping * (x - 4.0 * y))

    high, low = split(corr_ref[4])
    total = g_ref[...] + dot(jnp.concatenate([high, low], axis=1), cell_edge[...])

    turn_ref[...] = jnp.concatenate([total, pltpu.roll(total, NK - 1, 1)], axis=0).T
    for i in range(half):
        outgoing[:, i, :] = turn_ref[pl.ds(2 * i, n_pitch, stride=handoff), :]

    line = min(8, n_pitch)

    def send(k, carry):
        q = (k % (n_pitch // line)) * line + k // (n_pitch // line)

        @pl.when(q != p)
        def _():
            pltpu.make_async_remote_copy(
                outgoing.at[q],
                arrived.at[p],
                wall_send,
                wall_recv,
                device_id=(r, q, s),
                device_id_type=MESH,
            ).start()

        return carry

    lax.fori_loop(0, n_pitch, send, 0)
    pltpu.make_async_copy(outgoing.at[p], arrived.at[p], wall_recv).start()

    for e, at_row in enumerate((0, 1, NJ - 2, NJ - 1)):
        rows = pl.ds(at_row, TC, stride=NJ)
        upd_ref[rows, :] = upd_ref[rows, :] + corr_ref[e, 0:TC, :]
    e_lane = iota((2 * NS, NS), 0) & 3
    to_column = one_hot(iota((2 * NS, NS), 1) == jnp.where(e_lane < 2, e_lane, NS - 4 + e_lane))
    own = lane // 4 == iota((NJ, NS), 0)
    for t in range(NT):
        spread = jnp.concatenate(
            [
                jnp.where(own, corr_ref[4, t * NC + c : t * NC + c + 1, :], 0.0)
                for c in range(NC)
            ],
            axis=0,
        )
        high, low = split(spread)
        rows = slice(t * NC * NJ, (t + 1) * NC * NJ)
        upd_ref[rows, :] = upd_ref[rows, :] + dot(
            jnp.concatenate([high, low], axis=1), to_column
        )

    pltpu.make_async_copy(arrived, arrived, wall_recv).wait()
    some = outgoing.at[pl.ds(0, n_pitch - 1)]
    pltpu.make_async_copy(some, some, wall_send).wait()
    for copy in halos + spectra:
        copy.wait_send()

    @pl.when(s < n_span - 1)
    def _():
        right.wait_send()

    @pl.when(s > 0)
    def _():
        left.wait_send()


def finish(sizes, upd_ref, arrived, slot_ref, out_hbm, wall_ref, sem):
    half = NK // sizes[1] // 2
    stores = []
    for i in range(PARTS):
        part = pl.ds(i * (ROWS // PARTS), ROWS // PARTS)
        copy = pltpu.make_async_copy(upd_ref.at[part], out_hbm.at[part], sem.at[i])
        copy.start()
        stores.append(copy)

    slots = jnp.concatenate([arrived[:, i, :] for i in range(half)], axis=0).T
    high, low = split(jnp.concatenate([slots[0:PAD], slots[PAD : 2 * PAD]], axis=1))
    placed = dot(jnp.concatenate([high, low], axis=0), slot_ref[...])
    placed = placed[0:PAD] + placed[PAD : 2 * PAD]
    for k in range(NK // NS):
        wall_ref[:, k, :] = placed[0:TC, k * NS : (k + 1) * NS]
    for copy in stores:
        copy.wait()


def local(sizes, unknowns, spectrum, blades, harmonics, pitch_jac, span_jac, send_cell, recv_order):
    n_row, n_pitch, n_span = sizes
    half = NK // n_pitch // 2
    vmem, dma = pltpu.VMEM, pltpu.SemaphoreType.DMA
    in_hbm = pl.BlockSpec(memory_space=pltpu.HBM)
    in_vmem = pl.BlockSpec(memory_space=pltpu.VMEM)
    smem = pltpu.SMEM
    updated, arrived, slots = pl.pallas_call(
        functools.partial(section, sizes),
        out_shape=(vmem((ROWS, NS), F32), vmem((n_pitch, half, NS), F32), vmem((NK, NK), BF16)),
        in_specs=[in_hbm] * 8,
        out_specs=(in_vmem, in_vmem, in_vmem),
        scratch_shapes=[
            smem((n_row,), I32),
            smem((n_row, H), I32),
            smem((NC, NC), F32),
            smem((NC, NC), F32),
            vmem((ROWS, NS), F32),
            vmem((NT * NJ, NC * NS), F32),
            vmem((n_row, H * NC, 2, NS), F32),
            vmem((PAD, NC * NS), F32),
            vmem((4 * PAD, NC * NS), BF16),
            vmem((NT * NJ, 2 * NS), BF16),
            vmem((1, NK), I32),
            vmem((1, NK), I32),
            vmem((2 * NS, NK), BF16),
            vmem((NJ, NK), F32),
            vmem((2 * NS, NK), BF16),
            vmem((PAD, 2 * NS), BF16),
            vmem((PAD, 2 * NS), BF16),
            vmem((2, 2, PAD, NS), F32),
            vmem((2, 2, PAD, NS), F32),
            vmem((2, PAD // 2, NS), F32),
            vmem((2, PAD // 2, NS), F32),
            vmem((PAD, NS), F32),
            vmem((5, PAD, NS), F32),
            vmem((NT, NC, NK), F32),
            vmem((PAD, NK), F32),
            vmem((NK, NS), F32),
            vmem((n_pitch, half, NS), F32),
            dma((PARTS + 6,)),
            dma((2,)),
            dma((2,)),
            dma((2,)),
            dma((2,)),
            dma((n_row,)),
            dma,
            dma,
            dma,
            pltpu.SemaphoreType.REGULAR,
        ],
        compiler_params=pltpu.CompilerParams(
            collective_id=1, has_side_effects=True, vmem_limit_bytes=32 * 1024 * 1024
        ),
        name="flux_section",
    )(
        *(
            pltpu.with_memory_space_constraint(x, pltpu.HBM)
            for x in (
                blades,
                harmonics,
                pitch_jac,
                span_jac,
                unknowns.reshape(ROWS, NS),
                jnp.transpose(spectrum[0], (1, 2, 0, 3)).reshape(H * NC, 2, NS),
                send_cell.reshape(1, NK),
                recv_order.reshape(1, NK),
            )
        )
    )
    updated, wall = pl.pallas_call(
        functools.partial(finish, sizes),
        out_shape=(
            jax.ShapeDtypeStruct((ROWS, NS), F32),
            jax.ShapeDtypeStruct((TC, NK // NS, NS), F32),
        ),
        in_specs=[in_vmem] * 3,
        out_specs=(in_hbm, in_vmem),
        scratch_shapes=[dma((PARTS,))],
        compiler_params=pltpu.CompilerParams(vmem_limit_bytes=8 * 1024 * 1024),
        name="wall_order",
    )(updated, arrived, slots)
    return (
        updated.reshape(unknowns.shape),
        wall.reshape(1, 1, NT, NC, NK),
    )


def solution(mesh):
    sizes = (mesh.shape["row"], mesh.shape["pitch"], mesh.shape["span"])
    return jax.shard_map(
        functools.partial(local, sizes),
        mesh=mesh,
        in_specs=(
            P("row", None, None, "pitch", "span"),
            P("row", None, None, None, "span"),
            P(),
            P(),
            P(),
            P(),
            P("row", "span", "pitch", None),
            P("row", "span", "pitch", None),
        ),
        out_specs=(P("row", None, None, "pitch", "span"), P("row", "span", None, None, "pitch")),
        check_vma=False,
    )
```

```python
import functools
import math

import jax
import jax.numpy as jnp
import numpy as np
from jax import lax
from jax.experimental import pallas as pl
from jax.experimental.pallas import tpu as pltpu
from jax.sharding import PartitionSpec as P

MESH = pl.DeviceIdType.MESH
F32, BF16, I32 = jnp.float32, jnp.bfloat16, jnp.int32

H = 5
NT = 11
NC = 5
NJ = 32
NS = 128
NK = 256
TC = NT * NC
PAD = 64
ROWS = TC * NJ
PARTS = 5

step_size = 0.25
damping = 1.0 / 16.0
coupling = 0.5
frequency = 0.5
far_weight = 0.5

d_entries = [
    float(np.float32(0.5 * frequency * math.cos(math.pi * n) / math.sin(math.pi * n / NT)))
    for n in range(1, NT // 2 + 1)
]


def iota(shape, dim):
    return lax.broadcasted_iota(I32, shape, dim)


def split(x):
    high = x.astype(BF16)
    return high, (x - high.astype(F32)).astype(BF16)


def dot(a, b):
    return lax.dot_general(a, b, (((1,), (0,)), ((), ())), preferred_element_type=F32)


def one_hot(condition):
    return jnp.where(condition, 1.0, 0.0).astype(BF16)


def section(
    sizes,
    blades_hbm,
    harmonics_hbm,
    pitch_jac_hbm,
    span_jac_hbm,
    u_hbm,
    spec_hbm,
    cell_hbm,
    order_hbm,
    upd_ref,
    arrived,
    slot_ref,
    blades,
    harmonics,
    pitch_jac,
    span_jac,
    u_ref,
    heard_ref,
    specs,
    coeff_ref,
    rhs_ref,
    table_ref,
    cell_ref,
    order_ref,
    cell_s,
    cell_j,
    cell_edge,
    mix_p,
    mix_s,
    pitch_out,
    pitch_in,
    span_out,
    span_in,
    edge_ref,
    corr_ref,
    g_part,
    g_ref,
    turn_ref,
    outgoing,
    load_sem,
    pitch_send,
    pitch_recv,
    span_send,
    span_recv,
    row_send,
    row_recv,
    wall_send,
    wall_recv,
    answer,
):
    n_row, n_pitch, n_span = sizes
    handoff = NK // n_pitch
    half = handoff // 2
    r, p, s = lax.axis_index("row"), lax.axis_index("pitch"), lax.axis_index("span")

    def pitch_peer(k):
        return (r, lax.rem(p + k, n_pitch), s)

    def row_peer(k):
        return (lax.rem(r + k, n_row), p, s)

    loads = []
    for i in range(PARTS):
        part = pl.ds(i * (ROWS // PARTS), ROWS // PARTS)
        copy = pltpu.make_async_copy(u_hbm.at[part], u_ref.at[part], load_sem.at[i])
        copy.start()
        loads.append(copy)

    middle = n_span // 2
    mate = s + 1 - 2 * lax.rem(s, 2)
    below, above = s == middle - 1, s == middle

    def span_peer(k):
        return (r, p, lax.rem(s + k + n_span, n_span))

    barrier = pltpu.get_barrier_semaphore()
    pl.semaphore_signal(barrier, inc=1, device_id=(r, p, mate), device_id_type=MESH)

    @pl.when(below)
    def _():
        pl.semaphore_signal(barrier, inc=1, device_id=span_peer(1), device_id_type=MESH)

    for k in (1, n_pitch - 1):
        pl.semaphore_signal(barrier, inc=1, device_id=pitch_peer(k), device_id_type=MESH)
    for k in range(1, n_row):
        pl.semaphore_signal(barrier, inc=1, device_id=row_peer(k), device_id_type=MESH)

    def greet(k, carry):
        pl.semaphore_signal(barrier, inc=1, device_id=pitch_peer(k), device_id_type=MESH)
        return carry

    lax.fori_loop(2, n_pitch - 1, greet, 0)

    lane = iota((1, NS), 1)

    for copy in loads:
        copy.wait()
    edges = jnp.zeros((TC, NS), F32)
    for j in range(NJ):
        turned = pltpu.roll(u_ref[pl.ds(j, TC, stride=NJ), :], (2 + 4 * j) % NS, 1)
        edges = jnp.where((lane >= 4 * j) & (lane < 4 * j + 4), turned, edges)
    edge_ref[0:TC, :] = edges
    edge_ref[TC:PAD, :] = jnp.zeros((PAD - TC, NS), F32)
    e4 = lax.rem(lane, 4)
    low, high = edge_ref[0 : PAD // 2, :], edge_ref[PAD // 2 : PAD, :]
    span_out[0] = jnp.where(e4 < 2, low, pltpu.roll(high, 2, 1))
    span_out[1] = jnp.where(e4 >= 2, low, pltpu.roll(high, NS - 2, 1))

    greeters = 1 + n_row - 1 + n_pitch - 1
    pl.semaphore_wait(barrier, jnp.where(above, greeters + 1, greeters))

    @pl.when(above)
    def _():
        pl.semaphore_signal(answer, inc=1, device_id=span_peer(-1), device_id_type=MESH)

    right = pltpu.make_async_remote_copy(
        span_out.at[0],
        span_in.at[0],
        span_send.at[0],
        span_recv.at[0],
        device_id=span_peer(1),
        device_id_type=MESH,
    )
    left = pltpu.make_async_remote_copy(
        span_out.at[1],
        span_in.at[1],
        span_send.at[1],
        span_recv.at[1],
        device_id=span_peer(-1),
        device_id_type=MESH,
    )

    @pl.when(s > 0)
    def _():
        left.start()

    @pl.when((s < n_span - 1) & (s != middle - 1))
    def _():
        right.start()

    scalars = []
    for i, (src, dst) in enumerate(
        (
            (blades_hbm, blades),
            (harmonics_hbm, harmonics),
            (pitch_jac_hbm, pitch_jac),
            (span_jac_hbm, span_jac),
            (cell_hbm, cell_ref),
            (order_hbm, order_ref),
        )
    ):
        copy = pltpu.make_async_copy(src, dst, load_sem.at[PARTS + i])
        copy.start()
        scalars.append(copy)

    pitch_out[:, :, TC:PAD, :] = jnp.zeros((2, 2, PAD - TC, NS), F32)
    for layer in range(2):
        pitch_out[0, layer, 0:TC, :] = u_ref[pl.ds(NJ - 2 + layer, TC, stride=NJ), :]
        pitch_out[1, layer, 0:TC, :] = u_ref[pl.ds(layer, TC, stride=NJ), :]

    halos = []
    for way, k in ((0, 1), (1, n_pitch - 1)):
        copy = pltpu.make_async_remote_copy(
            pitch_out.at[way],
            pitch_in.at[way],
            pitch_send.at[way],
            pitch_recv.at[way],
            device_id=pitch_peer(k),
            device_id_type=MESH,
        )
        halos.append(copy)

    @pl.when(s < middle)
    def _():
        for copy in halos:
            copy.start()

    spectra = []
    for k in range(1, n_row):
        copy = pltpu.make_async_remote_copy(
            spec_hbm,
            specs.at[r],
            row_send.at[k],
            row_recv,
            device_id=row_peer(k),
            device_id_type=MESH,
        )
        copy.start()
        spectra.append(copy)
    pltpu.make_async_copy(spec_hbm, specs.at[r], row_recv).start()

    g_ref[TC:PAD, :] = jnp.zeros((PAD - TC, NK), F32)
    coeff_ref[...] = jnp.zeros_like(coeff_ref)

    @pl.when(s == 0)
    def _():
        span_in[0] = jnp.zeros_like(span_in[0])

    @pl.when(s == n_span - 1)
    def _():
        span_in[1] = jnp.zeros_like(span_in[1])

    for copy in scalars:
        copy.wait()
    cell = cell_ref[...]
    cj, cs = cell // NS, lax.rem(cell, NS)
    cell_s[...] = one_hot((iota((2 * NS, NK), 0) & (NS - 1)) == cs)
    cell_j[...] = jnp.where(iota((NJ, NK), 0) == cj, 1.0, 0.0)
    place = iota((2 * NS, NK), 0) & (NS - 1)
    e_row = place & 3
    column = jnp.where(e_row < 2, e_row, NS - 4 + e_row)
    cell_edge[...] = one_hot((place // 4 == cj) & (column == cs))
    rho = iota((NK, NK), 0)
    rest = rho & (NS - 1)
    slot = (rest & (n_pitch - 1)) * handoff + (rest // n_pitch) * 2 + rho // NS
    slot_ref[...] = one_hot(slot == order_ref[...])

    mr, mc = iota((PAD, NS), 0), iota((PAD, NS), 1) & (PAD - 1)
    tr, tcol = (mr * 205) >> 10, (mc * 205) >> 10
    cr, cc = mr - 5 * tr, mc - 5 * tcol
    same = (tr == tcol) & (mr < TC) & (mc < TC)
    pair = jnp.where(same, cr * NC + cc, -1)
    for jac, mix in ((pitch_jac, mix_p), (span_jac, mix_s)):
        m = jnp.zeros((PAD, NS), F32)
        for a in range(NC):
            for c in range(NC):
                m = jnp.where(pair == a * NC + c, jac[a, c], m)
        mh, ml = split(m)
        mix[:, 0:NS] = mh
        mix[:, NS : 2 * NS] = ml

    l64 = lane & (PAD - 1)
    lg, lk = l64 // 16, l64 & 15
    order_of = jnp.zeros((1, NS), I32)
    turns_of = jnp.zeros((1, NS), I32)
    weight = jnp.zeros((1, NS), F32)
    for g in range(n_row):
        distance = jnp.abs(r - g)
        w = jnp.where(distance == 1, 1.0, jnp.where(distance >= 2, far_weight, 0.0)).astype(F32)
        weight = jnp.where((lg == g) & (lk < 2 * H), w, weight)
        for n in range(H):
            here = (lg == g) & (lk // 2 == n)
            order_of = jnp.where(here, harmonics[g, n], order_of)
            turns_of = jnp.where(here, harmonics[g, n] * blades[g], turns_of)
    whole = n_pitch * NJ
    cells = p * NJ + iota((NJ, NS), 0)
    phase_j = ((turns_of * cells) & (whole - 1)).astype(F32) * (2.0 * math.pi / whole)
    phase_j = phase_j - (lk & 1).astype(F32) * (0.5 * math.pi)
    times = order_of * iota((16, NS), 0)
    times = times - NT * ((times * 5958) >> 16)
    phase_t = times.astype(F32) * (2.0 * math.pi / NT)
    cos_j, sin_j = weight * jnp.cos(phase_j), weight * jnp.sin(phase_j)
    cos_t, sin_t = jnp.cos(phase_t), jnp.sin(phase_t)
    for t in range(NT):
        high, low = split(cos_t[t : t + 1] * cos_j - sin_t[t : t + 1] * sin_j)
        table_ref[t * NJ : (t + 1) * NJ, 0:NS] = high
        table_ref[t * NJ : (t + 1) * NJ, NS : 2 * NS] = low

    row = iota((1, NJ, 1), 1)

    def at(t):
        return pl.ds(pl.multiple_of(t * (NC * NJ), NC * NJ), NC * NJ)

    def interior(t, carry):
        x = u_ref[at(t), :]
        m1 = jnp.where(lane >= 1, pltpu.roll(x, 1, 1), 0.0)
        m2 = jnp.where(lane >= 2, pltpu.roll(x, 2, 1), 0.0)
        p1 = jnp.where(lane < NS - 1, pltpu.roll(x, NS - 1, 1), 0.0)
        p2 = jnp.where(lane < NS - 2, pltpu.roll(x, NS - 2, 1), 0.0)
        d1s = (0.5 * (p1 - m1)).reshape(NC, NJ, NS)
        fourth = ((p2 + m2) - 4.0 * (p1 + m1)).reshape(NC, NJ, NS)
        x = x.reshape(NC, NJ, NS)
        m1 = jnp.where(row >= 1, pltpu.roll(x, 1, 1), 0.0)
        m2 = jnp.where(row >= 2, pltpu.roll(x, 2, 1), 0.0)
        p1 = jnp.where(row < NJ - 1, pltpu.roll(x, NJ - 1, 1), 0.0)
        p2 = jnp.where(row < NJ - 2, pltpu.roll(x, NJ - 2, 1), 0.0)
        d1p = 0.5 * (p1 - m1)
        fourth = fourth + ((p2 + m2) - 4.0 * (p1 + m1))
        change = damping * fourth + (12.0 * damping + 2.0 * coupling) * x
        for n in range(1, NT // 2 + 1):
            before = u_ref[at(lax.rem(t + NT - n, NT)), :]
            after = u_ref[at(lax.rem(t + n, NT)), :]
            change = change + d_entries[n - 1] * (before - after).reshape(NC, NJ, NS)
        for a in range(NC):
            flux = change[a]
            for c in range(NC):
                flux = flux + pitch_jac[a, c] * d1p[c] + span_jac[a, c] * d1s[c]
            upd_ref[pl.ds(pl.multiple_of((t * NC + a) * NJ, NJ), NJ), :] = x[a] - step_size * flux
        return carry

    lax.fori_loop(0, NT, interior, 0)

    pltpu.make_async_copy(specs, specs, row_recv).wait()
    for g in range(n_row):
        for n in range(H):
            for c in range(NC):
                coeff_ref[16 * g + 2 * n : 16 * g + 2 * n + 2, c * NS : (c + 1) * NS] = specs[
                    g, n * NC + c
                ]
    high, low = split(coeff_ref[...])
    for k in range(2):
        rhs_ref[2 * PAD * k : 2 * PAD * k + PAD, :] = high
        rhs_ref[2 * PAD * k + PAD : 2 * PAD * (k + 1), :] = low
    heard_ref[...] = dot(table_ref[...], rhs_ref[...])

    def gather(t, carry):
        heard = heard_ref[pl.ds(pl.multiple_of(t * NJ, NJ), NJ), :]
        heard = jnp.concatenate([heard[:, c * NS : (c + 1) * NS] for c in range(NC)], axis=0)
        x = upd_ref[at(t), :] + (step_size * coupling) * heard
        upd_ref[at(t), :] = x
        high, low = split(x)
        found = dot(jnp.concatenate([high, low], axis=1), cell_s[...])
        found = found.reshape(NC, NJ, NK) * cell_j[...]
        g_part[t] = jnp.sum(found, axis=1)
        return carry

    lax.fori_loop(0, NT, gather, 0)

    @pl.when(s >= middle)
    def _():
        for copy in halos:
            copy.start()

    for t in range(NT):
        g_ref[t * NC : (t + 1) * NC, :] = g_part[t]

    for copy in halos:
        copy.wait_recv()
    inner = jnp.concatenate([pitch_in[0, 1], pitch_in[1, 0]], axis=1)
    high, low = split(inner)
    mixed = dot(mix_p[...], jnp.concatenate([high, low, high, low], axis=0))
    corr_ref[0] = -step_size * (
        -0.5 * mixed[:, 0:NS] + damping * (pitch_in[0, 0] - 4.0 * pitch_in[0, 1])
    )
    corr_ref[1] = (-step_size * damping) * pitch_in[0, 1]
    corr_ref[2] = (-step_size * damping) * pitch_in[1, 0]
    corr_ref[3] = -step_size * (
        0.5 * mixed[:, NS : 2 * NS] + damping * (pitch_in[1, 1] - 4.0 * pitch_in[1, 0])
    )

    high, low = split(corr_ref[0:4].reshape(4 * PAD, NS))
    found = dot(jnp.concatenate([high, low], axis=1), cell_s[...])
    total = g_ref[...]
    for e, at_row in enumerate((0, 1, NJ - 2, NJ - 1)):
        total = total + found[e * PAD : (e + 1) * PAD] * cell_j[at_row : at_row + 1, :]
    g_ref[...] = total

    @pl.when(below)
    def _():
        pl.semaphore_wait(answer, 1)
        right.start()

    @pl.when(s < n_span - 1)
    def _():
        left_in = pltpu.make_async_copy(span_in.at[1], span_in.at[1], span_recv.at[1])
        left_in.wait()

    @pl.when(s > 0)
    def _():
        right_in = pltpu.make_async_copy(span_in.at[0], span_in.at[0], span_recv.at[0])
        right_in.wait()

    from_left, from_right = span_in[0], span_in[1]
    x = jnp.concatenate(
        [
            jnp.where(e4 < 2, from_left, from_right),
            jnp.where(e4 < 2, pltpu.roll(from_left, NS - 2, 1), pltpu.roll(from_right, 2, 1)),
        ],
        axis=0,
    )
    y = jnp.where(e4 == 0, pltpu.roll(x, NS - 1, 1), jnp.where(e4 == 3, pltpu.roll(x, 1, 1), 0.0))
    sign = jnp.where(e4 == 0, -0.5, jnp.where(e4 == 3, 0.5, 0.0))
    high, low = split(y)
    mixed = dot(mix_s[...], jnp.concatenate([high, low, high, low], axis=0))
    corr_ref[4] = -step_size * (sign * mixed + damping * (x - 4.0 * y))

    high, low = split(corr_ref[4])
    total = g_ref[...] + dot(jnp.concatenate([high, low], axis=1), cell_edge[...])

    turn_ref[...] = jnp.concatenate([total, pltpu.roll(total, NK - 1, 1)], axis=0).T
    for i in range(half):
        outgoing[:, i, :] = turn_ref[pl.ds(2 * i, n_pitch, stride=handoff), :]

    line = min(8, n_pitch)

    def send(k, carry):
        q = (k % (n_pitch // line)) * line + k // (n_pitch // line)

        @pl.when(q != p)
        def _():
            pltpu.make_async_remote_copy(
                outgoing.at[q],
                arrived.at[p],
                wall_send,
                wall_recv,
                device_id=(r, q, s),
                device_id_type=MESH,
            ).start()

        return carry

    lax.fori_loop(0, n_pitch, send, 0)
    pltpu.make_async_copy(outgoing.at[p], arrived.at[p], wall_recv).start()

    for e, at_row in enumerate((0, 1, NJ - 2, NJ - 1)):
        rows = pl.ds(at_row, TC, stride=NJ)
        upd_ref[rows, :] = upd_ref[rows, :] + corr_ref[e, 0:TC, :]
    e_lane = iota((2 * NS, NS), 0) & 3
    to_column = one_hot(iota((2 * NS, NS), 1) == jnp.where(e_lane < 2, e_lane, NS - 4 + e_lane))
    own = lane // 4 == iota((NJ, NS), 0)
    for t in range(NT):
        spread = jnp.concatenate(
            [
                jnp.where(own, corr_ref[4, t * NC + c : t * NC + c + 1, :], 0.0)
                for c in range(NC)
            ],
            axis=0,
        )
        high, low = split(spread)
        rows = slice(t * NC * NJ, (t + 1) * NC * NJ)
        upd_ref[rows, :] = upd_ref[rows, :] + dot(
            jnp.concatenate([high, low], axis=1), to_column
        )

    pltpu.make_async_copy(arrived, arrived, wall_recv).wait()
    some = outgoing.at[pl.ds(0, n_pitch - 1)]
    pltpu.make_async_copy(some, some, wall_send).wait()
    for copy in halos + spectra:
        copy.wait_send()

    @pl.when(s < n_span - 1)
    def _():
        right.wait_send()

    @pl.when(s > 0)
    def _():
        left.wait_send()


def finish(sizes, upd_ref, arrived, slot_ref, out_hbm, wall_ref, sem):
    half = NK // sizes[1] // 2
    stores = []
    for i in range(PARTS):
        part = pl.ds(i * (ROWS // PARTS), ROWS // PARTS)
        copy = pltpu.make_async_copy(upd_ref.at[part], out_hbm.at[part], sem.at[i])
        copy.start()
        stores.append(copy)

    slots = jnp.concatenate([arrived[:, i, :] for i in range(half)], axis=0).T
    high, low = split(jnp.concatenate([slots[0:PAD], slots[PAD : 2 * PAD]], axis=1))
    placed = dot(jnp.concatenate([high, low], axis=0), slot_ref[...])
    placed = placed[0:PAD] + placed[PAD : 2 * PAD]
    for k in range(NK // NS):
        wall_ref[:, k, :] = placed[0:TC, k * NS : (k + 1) * NS]
    for copy in stores:
        copy.wait()


def local(sizes, unknowns, spectrum, blades, harmonics, pitch_jac, span_jac, send_cell, recv_order):
    n_row, n_pitch, n_span = sizes
    half = NK // n_pitch // 2
    vmem, dma = pltpu.VMEM, pltpu.SemaphoreType.DMA
    in_hbm = pl.BlockSpec(memory_space=pltpu.HBM)
    in_vmem = pl.BlockSpec(memory_space=pltpu.VMEM)
    smem = pltpu.SMEM
    updated, arrived, slots = pl.pallas_call(
        functools.partial(section, sizes),
        out_shape=(vmem((ROWS, NS), F32), vmem((n_pitch, half, NS), F32), vmem((NK, NK), BF16)),
        in_specs=[in_hbm] * 8,
        out_specs=(in_vmem, in_vmem, in_vmem),
        scratch_shapes=[
            smem((n_row,), I32),
            smem((n_row, H), I32),
            smem((NC, NC), F32),
            smem((NC, NC), F32),
            vmem((ROWS, NS), F32),
            vmem((NT * NJ, NC * NS), F32),
            vmem((n_row, H * NC, 2, NS), F32),
            vmem((PAD, NC * NS), F32),
            vmem((4 * PAD, NC * NS), BF16),
            vmem((NT * NJ, 2 * NS), BF16),
            vmem((1, NK), I32),
            vmem((1, NK), I32),
            vmem((2 * NS, NK), BF16),
            vmem((NJ, NK), F32),
            vmem((2 * NS, NK), BF16),
            vmem((PAD, 2 * NS), BF16),
            vmem((PAD, 2 * NS), BF16),
            vmem((2, 2, PAD, NS), F32),
            vmem((2, 2, PAD, NS), F32),
            vmem((2, PAD // 2, NS), F32),
            vmem((2, PAD // 2, NS), F32),
            vmem((PAD, NS), F32),
            vmem((5, PAD, NS), F32),
            vmem((NT, NC, NK), F32),
            vmem((PAD, NK), F32),
            vmem((NK, NS), F32),
            vmem((n_pitch, half, NS), F32),
            dma((PARTS + 6,)),
            dma((2,)),
            dma((2,)),
            dma((2,)),
            dma((2,)),
            dma((n_row,)),
            dma,
            dma,
            dma,
            pltpu.SemaphoreType.REGULAR,
        ],
        compiler_params=pltpu.CompilerParams(
            collective_id=1, has_side_effects=True, vmem_limit_bytes=32 * 1024 * 1024
        ),
        name="flux_section",
    )(
        *(
            pltpu.with_memory_space_constraint(x, pltpu.HBM)
            for x in (
                blades,
                harmonics,
                pitch_jac,
                span_jac,
                unknowns.reshape(ROWS, NS),
                jnp.transpose(spectrum[0], (1, 2, 0, 3)).reshape(H * NC, 2, NS),
                send_cell.reshape(1, NK),
                recv_order.reshape(1, NK),
            )
        )
    )
    updated, wall = pl.pallas_call(
        functools.partial(finish, sizes),
        out_shape=(
            jax.ShapeDtypeStruct((ROWS, NS), F32),
            jax.ShapeDtypeStruct((TC, NK // NS, NS), F32),
        ),
        in_specs=[in_vmem] * 3,
        out_specs=(in_hbm, in_vmem),
        scratch_shapes=[dma((PARTS,))],
        compiler_params=pltpu.CompilerParams(vmem_limit_bytes=8 * 1024 * 1024),
        name="wall_order",
    )(updated, arrived, slots)
    return (
        updated.reshape(unknowns.shape),
        wall.reshape(1, 1, NT, NC, NK),
    )


def solution(mesh):
    sizes = (mesh.shape["row"], mesh.shape["pitch"], mesh.shape["span"])
    return jax.shard_map(
        functools.partial(local, sizes),
        mesh=mesh,
        in_specs=(
            P("row", None, None, "pitch", "span"),
            P("row", None, None, None, "span"),
            P(),
            P(),
            P(),
            P(),
            P("row", "span", "pitch", None),
            P("row", "span", "pitch", None),
        ),
        out_specs=(P("row", None, None, "pitch", "span"), P("row", "span", None, None, "pitch")),
        check_vma=False,
    )
```
